512 devices in a mesh: seq: 64 (over x, y, core), head: 8 (over z).
Axes of the slice: x: 4, y: 8, z: 8, core: 2. Of those that a mesh axis runs over, the one named last changes fastest.
Arguments:
- queries: bfloat16 [65536, 4096], P(('seq', 'head')), may hold values from -80 to 80
- keys: bfloat16 [65536, 512], P(('seq', 'head')), may hold values from -4 to 4
- values: bfloat16 [65536, 512], P(('seq', 'head')), may hold values from -6 to 6
- output_gradient: bfloat16 [65536, 4096], P(('seq', 'head')), may hold values from -0.59765625 to 0.59765625
- inputs: bfloat16 [65536, 8192], P(('seq', 'head')), may hold values from -6 to 6
- adapter_activation: bfloat16 [65536, 16], P(('seq', 'head')), may hold values from -6 to 6
- adapter_up_weight: bfloat16 [64, 16, 4096], P('seq', None, 'head'), may hold values from -0.09375 to 0.09375
- segment_length: int32 [64, 8], P('seq'), may hold values from 1 to 384, 1024 in all within a row
- segment_adapter: int32 [64, 8], P('seq'), may hold values from 0 to 63
- owner: int32 [64], replicated, may hold values from 0 to 63, each once
Outputs:
- down_gradient: float32 [64, 8192, 16], P('seq', 'head')
- up_gradient: float32 [64, 16, 4096], P('seq', None, 'head')
The draws below stay inside these ranges and needn't reach their ends.
Inputs may be any that keep to these rules, and one draw needn't show every extreme that they name: `segment_length`: each pack's 8 lengths sum to 1024, and its longest segment has exactly 384 tokens. `owner`: each seq index owns exactly one adapter.
All inputs are finite; a program needn't handle non-finite values.
Results may differ from the reference program's by a relative error of at most 0.014.
Values may be sent and summed in bfloat16 or wider, within the bound.
A program may use at most 64 MiB of HBM per device.

```python
import math
import jax
import jax.numpy as jnp
import numpy as np
from jax import lax

D = 8192
QUERY_HEADS = 32
KEY_VALUE_HEADS = 4
HEAD_SIZE = 128
ADAPTER_RANK = 16
PACK_SEGMENTS = 8
PACK_TOKENS = 1024
MOST = 384
ADAPTER_COUNT = 64
TOKEN_TOTAL = 65536
N_SEQ = 64


def key_base(key):
    return jnp.clip(jax.random.normal(key, (TOKEN_TOTAL, KEY_VALUE_HEADS * HEAD_SIZE), jnp.float32), -4.0, 4.0)


def draw_keys(key, part):
    common_rows = key_base(key)
    return common_rows.astype(jnp.bfloat16)


def draw_queries(key, part):
    key = jax.random.fold_in(key, 13)
    fresh_rows = jnp.clip(jax.random.normal(key, (TOKEN_TOTAL, QUERY_HEADS, HEAD_SIZE), jnp.float32), -4.0, 4.0)
    return fresh_rows.reshape(TOKEN_TOTAL, QUERY_HEADS * HEAD_SIZE).astype(jnp.bfloat16)


def with_ends(array, key, least, high):
    spot = [jax.random.randint(jax.random.fold_in(key, axis), (), 0, length) for axis, length in enumerate(array.shape)]
    longest = array.shape.index(max(array.shape))
    neighbour = spot[:longest] + [(spot[longest] + 1) % array.shape[longest]] + spot[longest + 1:]
    return array.at[tuple(spot)].set(least).at[tuple(neighbour)].set(high)


def level_of(stream_key, extent, cuts, smallest, high):
    loudness, own = 1.0, jax.random.fold_in(stream_key, 6)
    for axis_at, shards_of in cuts:
        draws = jnp.exp(jax.random.uniform(jax.random.fold_in(own, axis_at), (shards_of,), jnp.float32, smallest / len(cuts), high / len(cuts)))
        loudness = loudness * jnp.repeat(draws, extent[axis_at] // shards_of).reshape([-1 if axis == axis_at else 1 for axis in range(len(extent))])
    return loudness


def split_up(amount, total, most, skew):
    portions = [(1 << 20) // math.isqrt(rank ** skew) + 1 for rank in range(2, amount + 1)]
    surplus, counts = total - most - (amount - 1), [1] * (amount - 1)
    while surplus > 0:
        free = [i for i in range(amount - 1) if counts[i] < most]
        pool, budget = sum([portions[i] for i in free]), surplus
        for i in free:
            extra = min(most - counts[i], max(1, budget * portions[i] // pool), surplus)
            counts[i] = counts[i] + extra
            surplus = surplus - extra
    return np.array([most] + counts)


def uneven_parts(rng, count, total, bound, skew):
    if count == 2:
        one = jax.random.randint(rng, (), max(1, total - bound), min(bound, total - 1) + 1)
        return jnp.stack([one, total - one])
    lengths = jnp.asarray(split_up(count, total, bound, skew), jnp.int32)
    pairs = (count - 1) // 2
    source_of, taker = lengths[1:1 + 2 * pairs:2], lengths[2:2 + 2 * pairs:2]
    room = jnp.minimum(source_of - 1, bound - taker)
    moved = jax.random.randint(jax.random.fold_in(rng, 1), (pairs,), 0, 1 << 20) % (room + 1)
    lengths = lengths.at[1:1 + 2 * pairs:2].set(source_of - moved).at[2:2 + 2 * pairs:2].set(taker + moved)
    return lengths[jax.random.permutation(jax.random.fold_in(rng, 2), count)]


def bell_draw(stream_key, dims, width, most, cuts=(), held_as=jnp.bfloat16):
    entries = width * jax.random.normal(stream_key, dims, jnp.float32)
    if cuts:
        entries = entries * level_of(stream_key, dims, cuts, -0.22, 0.18)
    return jnp.clip(entries, -most, most).astype(held_as)


def setup_inputs(seed: int = 0) -> dict:
    seeds = jax.random.split(jax.random.key(seed), 11)
    return {
        "queries": draw_queries(jax.random.fold_in(seeds[10], 71), 0),
        "keys": draw_keys(jax.random.fold_in(seeds[10], 71), 0),
        "values": bell_draw(seeds[2], (TOKEN_TOTAL, KEY_VALUE_HEADS * HEAD_SIZE), 1.0, 6.0, ((0, 512),)),
        "output_gradient": bell_draw(seeds[3], (TOKEN_TOTAL, QUERY_HEADS * HEAD_SIZE), 0.1, 0.59765625, ((0, 512),)),
        "inputs": bell_draw(seeds[4], (TOKEN_TOTAL, D), 1.0, 6.0, ((0, 512),)),
        "adapter_activation": bell_draw(seeds[5], (TOKEN_TOTAL, ADAPTER_RANK), 1.0, 6.0, ((0, 512),)),
        "adapter_up_weight": bell_draw(seeds[6], (ADAPTER_COUNT, ADAPTER_RANK, QUERY_HEADS * HEAD_SIZE), (QUERY_HEADS * HEAD_SIZE) ** -0.5, 0.09375, ((0, 64), (2, 8))),
        "segment_length": jax.vmap(lambda own: uneven_parts(own, PACK_SEGMENTS, PACK_TOKENS, MOST, 2))(jax.random.split(seeds[7], N_SEQ)).reshape((N_SEQ, PACK_SEGMENTS)).astype(jnp.int32),
        "segment_adapter": with_ends(jax.random.randint(seeds[8], (N_SEQ, PACK_SEGMENTS), 0, ADAPTER_COUNT), jax.random.fold_in(seeds[8], 1), 0, ADAPTER_COUNT - 1).astype(jnp.int32),
        "owner": jax.random.permutation(seeds[9], ADAPTER_COUNT).astype(jnp.int32),
    }


ADAPTER_SCALE = 2.0
HIGHEST = lax.Precision.HIGHEST


def segment_of(seg_lens, pack_len):
    seg_ends = jnp.cumsum(seg_lens)
    positions = jnp.arange(pack_len, dtype=jnp.int32)
    return jnp.sum((positions[:, None] >= seg_ends[None, :]).astype(jnp.int32), axis=1)


def head_backward(q_head, g_head, k_head, v_head, segment):
    pack_len, head_width = q_head.shape
    score_scale = 1.0 / (head_width ** 0.5)
    positions = jnp.arange(pack_len, dtype=jnp.int32)
    k_wide = k_head.astype(jnp.float32)
    scores = jnp.dot(q_head.astype(jnp.float32), k_wide.T, preferred_element_type=jnp.float32) * score_scale
    allowed = (segment[:, None] == segment[None, :]) & (positions[None, :] <= positions[:, None])
    scores = jnp.where(allowed, scores, -jnp.inf)
    row_max = jnp.max(scores, axis=1, keepdims=True)
    weights = jnp.exp(scores - row_max)
    attn_prob = weights / jnp.sum(weights, axis=1, keepdims=True)
    d_prob = jnp.dot(g_head.astype(jnp.float32), v_head.astype(jnp.float32).T, preferred_element_type=jnp.float32)
    row_delta = jnp.sum(attn_prob * d_prob, axis=1, keepdims=True)
    dscore = (attn_prob * (d_prob - row_delta) * score_scale).astype(jnp.bfloat16)
    return jnp.dot(dscore.astype(jnp.float32), k_wide, preferred_element_type=jnp.float32).astype(jnp.bfloat16)


def reference(queries, keys, values, output_gradient, inputs, adapter_activation, adapter_up_weight, segment_length, segment_adapter, owner):
    query_group_width = QUERY_HEADS // KEY_VALUE_HEADS
    query_width = QUERY_HEADS * HEAD_SIZE

    def one_pack(totals, pack_index):
        down_running_sum, up_running_sum = totals
        starting_row = pack_index * PACK_TOKENS
        q_rows = lax.dynamic_slice_in_dim(queries, starting_row, PACK_TOKENS, 0).reshape(PACK_TOKENS, QUERY_HEADS, HEAD_SIZE).transpose(1, 0, 2)
        g_rows = lax.dynamic_slice_in_dim(output_gradient, starting_row, PACK_TOKENS, 0).reshape(PACK_TOKENS, QUERY_HEADS, HEAD_SIZE).transpose(1, 0, 2)
        key_rows = lax.dynamic_slice_in_dim(keys, starting_row, PACK_TOKENS, 0).reshape(PACK_TOKENS, KEY_VALUE_HEADS, HEAD_SIZE).transpose(1, 0, 2)
        value_rows = lax.dynamic_slice_in_dim(values, starting_row, PACK_TOKENS, 0).reshape(PACK_TOKENS, KEY_VALUE_HEADS, HEAD_SIZE).transpose(1, 0, 2)
        x_rows = lax.dynamic_slice_in_dim(inputs, starting_row, PACK_TOKENS, 0)
        activation_rows = lax.dynamic_slice_in_dim(adapter_activation, starting_row, PACK_TOKENS, 0)
        key_rows = jnp.repeat(key_rows, query_group_width, axis=0)
        value_rows = jnp.repeat(value_rows, query_group_width, axis=0)
        segment = segment_of(segment_length[pack_index], PACK_TOKENS)
        segment_index = segment_adapter[pack_index]
        dq_stack = lax.map(lambda stacked: head_backward(stacked[0], stacked[1], stacked[2], stacked[3], segment),
                           (q_rows, g_rows, key_rows, value_rows))
        dquery = dq_stack.transpose(1, 0, 2).reshape(PACK_TOKENS, query_width)
        up_weight_segment = adapter_up_weight[segment_index].reshape(PACK_SEGMENTS * ADAPTER_RANK, query_width)
        rank_seg = jnp.dot(dquery.astype(jnp.float32), up_weight_segment.astype(jnp.float32).T, preferred_element_type=jnp.float32)
        seg_mask = segment[:, None] == jnp.arange(PACK_SEGMENTS, dtype=jnp.int32)[None, :]
        rank_grad = jnp.sum(rank_seg.reshape(PACK_TOKENS, PACK_SEGMENTS, ADAPTER_RANK) * seg_mask[:, :, None], axis=1)
        rank_low = rank_grad.astype(jnp.bfloat16)
        mask_low = seg_mask.astype(jnp.bfloat16)
        rank_cols = (mask_low[:, :, None] * rank_low[:, None, :]).reshape(PACK_TOKENS, PACK_SEGMENTS * ADAPTER_RANK)
        act_cols = (mask_low[:, :, None] * activation_rows[:, None, :]).reshape(PACK_TOKENS, PACK_SEGMENTS * ADAPTER_RANK)
        part_a = jnp.dot(x_rows.astype(jnp.float32).T, rank_cols.astype(jnp.float32),
                         preferred_element_type=jnp.float32).reshape(D, PACK_SEGMENTS, ADAPTER_RANK)
        part_b = jnp.dot(act_cols.astype(jnp.float32).T, dquery.astype(jnp.float32),
                         preferred_element_type=jnp.float32).reshape(PACK_SEGMENTS, ADAPTER_RANK, query_width)
        onehot = (segment_index[:, None] == jnp.arange(ADAPTER_COUNT, dtype=jnp.int32)[None, :]).astype(jnp.float32)
        down_running_sum = down_running_sum + jnp.einsum("dsr,sa->adr", part_a, onehot, precision=HIGHEST)
        up_running_sum = up_running_sum + jnp.einsum("srf,sa->arf", part_b, onehot, precision=HIGHEST)
        return (down_running_sum, up_running_sum), None

    zeros_init = (jnp.zeros((ADAPTER_COUNT, D, ADAPTER_RANK), jnp.float32), jnp.zeros((ADAPTER_COUNT, ADAPTER_RANK, query_width), jnp.float32))
    (down_running_sum, up_running_sum), unused = lax.scan(one_pack, zeros_init, jnp.arange(N_SEQ, dtype=jnp.int32))
    down_gradient = jnp.zeros_like(down_running_sum).at[owner].set(down_running_sum) * ADAPTER_SCALE
    up_gradient = jnp.zeros_like(up_running_sum).at[owner].set(up_running_sum) * ADAPTER_SCALE
    return down_gradient, up_gradient
```

```python
import functools

import jax
import jax.numpy as jnp
from jax import lax
from jax.experimental import pallas as pl
from jax.experimental.pallas import tpu as pltpu
from jax.sharding import PartitionSpec as P

MESH = pl.DeviceIdType.MESH
F32, BF16, I32 = jnp.float32, jnp.bfloat16, jnp.int32

NX, NY, NZ = 4, 8, 8
HEAD_SIZE = 128
KV_HEADS = 4
GROUP = 8
RANK = 16
SEGMENTS = 8
COLS = SEGMENTS * RANK
TOKENS = 128
HALO = 3
KEYS = (HALO + 1) * TOKENS
WIDTH = 512
ADAPTER_SCALE = 2.0
SCORE_SCALE = 1.0 / HEAD_SIZE**0.5


def nt(a, b):
    return lax.dot_general(a, b, (((1,), (1,)), ((), ())), preferred_element_type=F32)


def nn(a, b):
    return lax.dot_general(a, b, (((1,), (0,)), ((), ())), preferred_element_type=F32)


class RingSum:
    def __init__(self, size, me, peer, chunk, sent, landed, send_sem, recv_sem, right):
        self.size, self.me, self.peer, self.chunk = size, me, peer, chunk
        self.sent, self.landed = sent, landed
        self.send_sem, self.recv_sem = send_sem, recv_sem
        self.ways = ((1, right, 0), (-1, size - 1 - right, right))
        self.copies = {}

    def stage(self, step):
        for sign, hops, base in self.ways:
            if step >= hops:
                continue
            slot = base + step
            target = lax.rem(self.me + sign * (hops - step) + self.size, self.size)
            total = self.chunk(target)
            if step > 0:
                self.copies[slot - 1].wait_recv()
                total = total + self.landed(slot - 1)[...].astype(F32)
            self.sent(slot)[...] = total.astype(self.sent(slot).dtype)
            copy = pltpu.make_async_remote_copy(
                src_ref=self.sent(slot),
                dst_ref=self.landed(slot),
                send_sem=self.send_sem(slot),
                recv_sem=self.recv_sem(slot),
                device_id=self.peer(sign),
                device_id_type=MESH,
            )
            copy.start()
            self.copies[slot] = copy

    def final(self):
        total = self.chunk(self.me)
        for _, hops, base in self.ways:
            slot = base + hops - 1
            self.copies[slot].wait_recv()
            total = total + self.landed(slot)[...].astype(F32)
        return total

    def drain(self):
        for copy in self.copies.values():
            copy.wait_send()


def kernel(
    q_hbm,
    g_hbm,
    x_hbm,
    k_ref,
    v_ref,
    act_ref,
    w_ref,
    len_ref,
    ada_ref,
    own_ref,
    down_ref,
    up_ref,
    qv,
    gv,
    xv,
    kb,
    vb,
    bias,
    dq,
    wall,
    wz,
    act_cols,
    rank_cols,
    slots,
    meta_s,
    meta_r,
    zs,
    zr,
    eb,
    ys,
    yr,
    xs,
    xr,
    xs2,
    xr2,
    ys2,
    yr2,
    ty,
    tx,
    load_sem,
    kv_send,
    kv_recv,
    wy_send,
    wy_recv,
    wx_send,
    wx_recv,
    wc_send,
    wc_recv,
    wz_send,
    wz_recv,
    zr_send,
    zr_recv,
    e_send,
    e_recv,
    f_send,
    f_recv,
    s_send,
    s_recv,
    m_send,
    m_recv,
):
    s = lax.axis_index("seq")
    z = lax.axis_index("head")
    core = lax.rem(s, 2)
    y = lax.rem(s // 2, NY)
    x = s // (2 * NY)

    def at_z(d):
        return (s, lax.rem(z + d + NZ, NZ))

    def at_y(d):
        return (x * (2 * NY) + lax.rem(y + d + NY, NY) * 2 + core, z)

    def at_x(d):
        return (lax.rem(x + d + NX, NX) * (2 * NY) + y * 2 + core, z)

    partner = (s + 1 - 2 * core, z)

    loads = []
    for g in range(KV_HEADS):
        lanes = pl.ds(g * GROUP * HEAD_SIZE, GROUP * HEAD_SIZE)
        for i, (src, dst) in enumerate(((q_hbm, qv), (g_hbm, gv))):
            copy = pltpu.make_async_copy(src.at[:, lanes], dst.at[:, lanes], load_sem.at[2 * g + i])
            copy.start()
            loads.append(copy)
    x_load = pltpu.make_async_copy(x_hbm, xv, load_sem.at[2 * KV_HEADS])
    x_load.start()

    barrier = pltpu.get_barrier_semaphore()
    others = (
        [at_z(d) for d in (1, 2, 3, -1, -2, -3)]
        + [at_y(d) for d in range(1, NY)]
        + [at_x(d) for d in range(1, NX)]
        + [partner]
    )
    for other in others:
        pl.semaphore_signal(barrier, inc=1, device_id=other, device_id_type=MESH)
    pl.semaphore_wait(barrier, len(others))

    def remote(src, dst, send, recv, to):
        copy = pltpu.make_async_remote_copy(
            src_ref=src, dst_ref=dst, send_sem=send, recv_sem=recv, device_id=to, device_id_type=MESH
        )
        copy.start()
        return copy

    sends = []
    kv_copies = []
    for g in range(KV_HEADS):
        lanes = pl.ds(g * HEAD_SIZE, HEAD_SIZE)
        row = []
        for d in range(1, HALO + 1):
            rows = pl.ds((HALO - d) * TOKENS, TOKENS)
            for i, (src, dst) in enumerate(((k_ref, kb), (v_ref, vb))):
                at = (g * HALO + d - 1) * 2 + i
                row.append(
                    remote(src.at[:, lanes], dst.at[rows, lanes], kv_send.at[at], kv_recv.at[at], at_z(d))
                )
        kv_copies.append(row)
        sends += row

    place = core * (NX * NY) + x * NY + y
    wy = []
    for d in range(1, NY):
        wy.append(remote(w_ref.at[0], wall.at[place], wy_send.at[d], wy_recv.at[d], at_y(d)))
    sends += wy
    wall[place] = w_ref[0]

    ends, total = [], 0
    for i in range(SEGMENTS):
        total = total + len_ref[0, i]
        ends.append(total)
    starts = [0] + ends[:-1]
    lane = lax.broadcasted_iota(I32, (8, COLS), 1)
    slot = lax.rem(lane, RANK)
    for i in range(SEGMENTS):
        owner = own_ref[ada_ref[0, i]]
        slot = slot + jnp.where(lane // RANK == i, owner * RANK, 0)
    meta_s[...] = slot
    slots[:, 0:COLS] = slot
    meta = remote(meta_s, meta_r, m_send.at[0], m_recv.at[0], partner)
    sends.append(meta)

    kb[HALO * TOKENS : KEYS, :] = k_ref[...]
    vb[HALO * TOKENS : KEYS, :] = v_ref[...]

    first = z * TOKENS
    row_pos = first + lax.broadcasted_iota(I32, (TOKENS, 1), 0)
    row_start = jnp.zeros((TOKENS, 1), I32)
    for i in range(1, SEGMENTS):
        row_start = jnp.where(row_pos >= starts[i], starts[i], row_start)
    key_pos = first - HALO * TOKENS + lax.broadcasted_iota(I32, (TOKENS, KEYS), 1)
    allowed = (key_pos >= row_start) & (key_pos <= row_pos)
    bias[...] = jnp.where(allowed, 0.0, -1e30).astype(F32)

    col = lax.broadcasted_iota(I32, (COLS, 1), 0)
    col_start = jnp.zeros((COLS, 1), I32)
    col_end = jnp.zeros((COLS, 1), I32)
    col_row = lax.rem(col, RANK)
    for i in range(SEGMENTS):
        here = col // RANK == i
        col_start = jnp.where(here, starts[i], col_start)
        col_end = jnp.where(here, ends[i], col_end)
        adapter = ada_ref[0, i]
        adapter_row = (lax.rem(adapter, 2) * (NX * NY) + adapter // 2) * RANK
        col_row = col_row + jnp.where(here, adapter_row, 0)
    token = first + lax.broadcasted_iota(I32, (COLS, TOKENS), 1)
    mask = (token >= col_start) & (token < col_end)
    spread = lax.rem(lax.broadcasted_iota(I32, (COLS, RANK), 0), RANK) == lax.broadcasted_iota(
        I32, (COLS, RANK), 1
    )
    spread = jnp.where(spread, 1.0, 0.0).astype(BF16)
    act_cols[...] = jnp.where(mask, nn(spread, act_ref[...]), 0.0).astype(BF16)

    def attend(g):
        for i in range(2):
            loads[2 * g + i].wait()
        for copy in kv_copies[g]:
            copy.wait_recv()
        lanes = pl.ds(g * HEAD_SIZE, HEAD_SIZE)

        def head(h, carry):
            at = pl.ds(pl.multiple_of((g * GROUP + h) * HEAD_SIZE, HEAD_SIZE), HEAD_SIZE)
            keys, values = kb[:, lanes], vb[:, lanes]
            scores = nt(qv[:, at], keys) * SCORE_SCALE + bias[...]
            weights = jnp.exp(scores - jnp.max(scores, axis=1, keepdims=True))
            scale = 1.0 / jnp.sum(weights, axis=1, keepdims=True)
            d_prob = nt(gv[:, at], values)
            delta = jnp.sum(weights * d_prob, axis=1, keepdims=True) * scale
            dscore = (weights * (d_prob - delta) * (scale * SCORE_SCALE)).astype(BF16)
            dq[:, at] = nn(dscore, keys).astype(BF16)
            return carry

        lax.fori_loop(0, GROUP, head, 0, unroll=2)

    for copy in wy:
        copy.wait_recv()
    mine = core * (NX * NY)

    def block(d):
        return wall.at[pl.ds(mine + lax.rem(x - d + NX, NX) * NY, NY)]

    wx = [None]
    for d in range(1, NX):
        wx.append(remote(block(0), block(0), wx_send.at[d], wx_recv.at[d], at_x(d)))
    wc = [remote(block(0), block(0), wc_send.at[0], wc_recv.at[0], partner)]
    sends += wx[1:]

    attend(0)
    for d in range(1, NX):
        wx[d].wait_recv()
        wc.append(remote(block(d), block(d), wc_send.at[d], wc_recv.at[d], partner))
    sends += wc
    attend(1)

    for copy in wc:
        copy.wait_recv()
    pick = jnp.where(lax.broadcasted_iota(I32, (COLS, 2 * NX * NY * RANK), 1) == col_row, 1.0, 0.0)
    wz[z] = nn(pick.astype(BF16), wall[...].reshape(2 * NX * NY * RANK, WIDTH)).astype(BF16)
    wz_ways = ((1, 3, 0), (-1, 4, 3))
    wz_copies = {}

    def pass_on(step):
        for sign, hops, base in wz_ways:
            if step < hops:
                if step > 0:
                    wz_copies[base + step - 1].wait_recv()
                at = lax.rem(z - sign * step + NZ, NZ)
                wz_copies[base + step] = remote(
                    wz.at[at], wz.at[at], wz_send.at[base + step], wz_recv.at[base + step], at_z(sign)
                )

    pass_on(0)
    attend(2)
    pass_on(1)
    attend(3)
    pass_on(2)

    def part(c, rows):
        return nt(wz[rows], dq[:, pl.ds(pl.multiple_of(c * WIDTH, WIDTH), WIDTH)])

    def b_chunk(c):
        return nn(act_cols[...], dq[:, pl.ds(pl.multiple_of(c * WIDTH, WIDTH), WIDTH)])

    def a_chunk(j, c):
        return nn(rank_cols[...], xv[:, pl.ds(pl.multiple_of((2 * c + j) * WIDTH, WIDTH), WIDTH)])

    def z_sum(blk, chunk, right):
        return RingSum(
            NZ,
            z,
            at_z,
            chunk,
            lambda i: zs.at[blk, i],
            lambda i: zr.at[blk, i],
            lambda i: zr_send.at[blk, i],
            lambda i: zr_recv.at[blk, i],
            right,
        )

    zsum = [
        z_sum(0, b_chunk, 3),
        z_sum(1, functools.partial(a_chunk, 0), 4),
        z_sum(2, functools.partial(a_chunk, 1), 4),
    ]
    zsum[0].stage(0)
    pass_on(3)
    for i in (2, 6):
        wz_copies[i].wait_recv()
    sends += list(wz_copies.values())
    rank = part(0, 0)
    for c in range(1, NZ):
        rank = rank + part(c, c)
    rank_cols[...] = jnp.where(mask, rank, 0.0).astype(BF16)
    x_load.wait()

    e_copies = {}

    def to_partner(blk):
        eb[blk, 0:COLS] = zsum[blk].final().astype(BF16)
        e_copies[blk] = remote(
            eb.at[blk, pl.ds(0, COLS)],
            eb.at[blk, pl.ds(COLS, COLS)],
            e_send.at[blk],
            e_recv.at[blk],
            partner,
        )

    def y_chunk(blk, c):
        row = lax.broadcasted_iota(I32, (NX * RANK, 2 * COLS), 0)
        key = (row // RANK) * (2 * NY * RANK) + (c * 2 + core) * RANK + lax.rem(row, RANK)
        return nn(jnp.where(key == slots[0:1, :], 1.0, 0.0).astype(BF16), eb[blk])

    def x_chunk(blk, c):
        row = lax.broadcasted_iota(I32, (NY * RANK, 2 * COLS), 0)
        key = (c * 2 * NY + (row // RANK) * 2 + core) * RANK + lax.rem(row, RANK)
        return nn(jnp.where(key == slots[0:1, :], 1.0, 0.0).astype(BF16), eb[blk])

    def rows_of(buf, c):
        return buf[pl.ds(pl.multiple_of(c * RANK, RANK), RANK), :]

    def f_sems(blk):
        return (lambda i: f_send.at[blk, i]), (lambda i: f_recv.at[blk, i])

    def s_sems(blk):
        return (lambda i: s_send.at[blk, i]), (lambda i: s_recv.at[blk, i])

    def y_first(blk, at):
        one = RingSum(
            NY, y, at_y, functools.partial(y_chunk, blk),
            lambda i: ys.at[at, i], lambda i: yr.at[at, i], *f_sems(blk), 4,
        )
        two = RingSum(
            NX, x, at_x, lambda c: rows_of(ty.at[at], c),
            lambda i: xs2.at[at, i], lambda i: xr2.at[at, i], *s_sems(blk), 2,
        )
        return one, two, ty.at[at]

    def x_first(blk, at):
        one = RingSum(
            NX, x, at_x, functools.partial(x_chunk, blk),
            lambda i: xs.at[at, i], lambda i: xr.at[at, i], *f_sems(blk), 2,
        )
        two = RingSum(
            NY, y, at_y, lambda c: rows_of(tx.at[at], c),
            lambda i: ys2.at[at, i], lambda i: yr2.at[at, i], *s_sems(blk), 4,
        )
        return one, two, tx.at[at]

    seq_sum = [y_first(0, 0), x_first(1, 0), y_first(2, 1)]
    outs = [
        (up_ref, pl.ds(0, WIDTH)),
        (down_ref, pl.ds(0, WIDTH)),
        (down_ref, pl.ds(WIDTH, WIDTH)),
    ]

    for step in range(4):
        for blk in (0, 1, 2):
            if blk > 0 or step > 0:
                zsum[blk].stage(step)
    meta.wait_recv()
    slots[:, COLS : 2 * COLS] = meta_r[...]
    for blk in (0, 1, 2):
        to_partner(blk)
    for step in range(4):
        for blk in (0, 1, 2):
            if step == 0:
                e_copies[blk].wait_recv()
            one = seq_sum[blk][0]
            if step < one.ways[0][1]:
                one.stage(step)
    for blk in (1, 0, 2):
        one, two, held = seq_sum[blk]
        held[...] = one.final()
        two.stage(0)
    for step in range(1, 4):
        for blk in (1, 0, 2):
            two = seq_sum[blk][1]
            if step < two.ways[0][1]:
                two.stage(step)
    for blk in (0, 2, 1):
        ref, lanes = outs[blk]
        ref[:, lanes] = seq_sum[blk][1].final() * ADAPTER_SCALE

    for copy in sends + list(e_copies.values()):
        copy.wait_send()
    for ring in zsum:
        ring.drain()
    for one, two, _ in seq_sum:
        one.drain()
        two.drain()


def on_device(q, k, v, g, x, act, w, length, adapter, owner):
    vmem = pl.BlockSpec(memory_space=pltpu.VMEM)
    smem = pl.BlockSpec(memory_space=pltpu.SMEM)
    hbm = pl.BlockSpec(memory_space=pl.ANY)
    dma = pltpu.SemaphoreType.DMA
    ring = NZ - 1
    scratch = [
        pltpu.VMEM((TOKENS, KV_HEADS * GROUP * HEAD_SIZE), BF16),
        pltpu.VMEM((TOKENS, KV_HEADS * GROUP * HEAD_SIZE), BF16),
        pltpu.VMEM((TOKENS, x.shape[1]), BF16),
        pltpu.VMEM((KEYS, WIDTH), BF16),
        pltpu.VMEM((KEYS, WIDTH), BF16),
        pltpu.VMEM((TOKENS, KEYS), F32),
        pltpu.VMEM((TOKENS, KV_HEADS * GROUP * HEAD_SIZE), BF16),
        pltpu.VMEM((2 * NX * NY, RANK, WIDTH), BF16),
        pltpu.VMEM((NZ, COLS, WIDTH), BF16),
        pltpu.VMEM((COLS, TOKENS), BF16),
        pltpu.VMEM((COLS, TOKENS), BF16),
        pltpu.VMEM((8, 2 * COLS), I32),
        pltpu.VMEM((8, COLS), I32),
        pltpu.VMEM((8, COLS), I32),
        pltpu.VMEM((3, ring, COLS, WIDTH), BF16),
        pltpu.VMEM((3, ring, COLS, WIDTH), BF16),
        pltpu.VMEM((3, 2 * COLS, WIDTH), BF16),
        pltpu.VMEM((2, NY - 1, NX * RANK, WIDTH), BF16),
        pltpu.VMEM((2, NY - 1, NX * RANK, WIDTH), BF16),
        pltpu.VMEM((1, NX - 1, NY * RANK, WIDTH), BF16),
        pltpu.VMEM((1, NX - 1, NY * RANK, WIDTH), BF16),
        pltpu.VMEM((2, NX - 1, RANK, WIDTH), F32),
        pltpu.VMEM((2, NX - 1, RANK, WIDTH), F32),
        pltpu.VMEM((1, NY - 1, RANK, WIDTH), F32),
        pltpu.VMEM((1, NY - 1, RANK, WIDTH), F32),
        pltpu.VMEM((2, NX * RANK, WIDTH), F32),
        pltpu.VMEM((1, NY * RANK, WIDTH), F32),
        dma((2 * KV_HEADS + 1,)),
        dma((KV_HEADS * HALO * 2,)),
        dma((KV_HEADS * HALO * 2,)),
        dma((NY,)),
        dma((NY,)),
        dma((NX,)),
        dma((NX,)),
        dma((NX,)),
        dma((NX,)),
        dma((ring,)),
        dma((ring,)),
        dma((3, ring)),
        dma((3, ring)),
        dma((3,)),
        dma((3,)),
        dma((3, ring)),
        dma((3, ring)),
        dma((3, ring)),
        dma((3, ring)),
        dma((1,)),
        dma((1,)),
    ]
    down, up = pl.pallas_call(
        kernel,
        out_shape=(
            jax.ShapeDtypeStruct((RANK, 2 * WIDTH), F32),
            jax.ShapeDtypeStruct((RANK, WIDTH), F32),
        ),
        in_specs=[hbm, hbm, hbm, vmem, vmem, vmem, vmem, smem, smem, smem],
        out_specs=(vmem, vmem),
        scratch_shapes=scratch,
        compiler_params=pltpu.CompilerParams(
            collective_id=0, has_side_effects=True, vmem_limit_bytes=40 * 1024 * 1024
        ),
    )(q, g, x, k, v, act.T, w, length, adapter, owner)
    return down.T[None], up[None]


def solution(mesh):
    return jax.shard_map(
        on_device,
        mesh=mesh,
        in_specs=(
            P(("seq", "head"), None),
            P(("seq", "head"), None),
            P(("seq", "head"), None),
            P(("seq", "head"), None),
            P(("seq", "head"), None),
            P(("seq", "head"), None),
            P("seq", None, "head"),
            P("seq", None),
            P("seq", None),
            P(),
        ),
        out_specs=(P("seq", "head", None), P("seq", None, "head")),
        check_vma=False,
    )
```

```python
import functools

import jax
import jax.numpy as jnp
from jax import lax
from jax.experimental import pallas as pl
from jax.experimental.pallas import tpu as pltpu
from jax.sharding import PartitionSpec as P

MESH = pl.DeviceIdType.MESH
F32, BF16, I32 = jnp.float32, jnp.bfloat16, jnp.int32

NX, NY, NZ = 4, 8, 8
HEAD_SIZE = 128
KV_HEADS = 4
GROUP = 8
RANK = 16
PAIR = 2
SEGMENTS = 8
COLS = SEGMENTS * RANK
TOKENS = 128
HALO = 3
KEYS = (HALO + 1) * TOKENS
WIDTH = 512
PIECE = 256
PIECES = 6
BEGIN = (-1, -1, 0, 0, 0, 0)
Y_FIRST = (0, 2)
ADAPTER_SCALE = 2.0
SCORE_SCALE = 1.0 / HEAD_SIZE**0.5


def nt(a, b):
    return lax.dot_general(a, b, (((1,), (1,)), ((), ())), preferred_element_type=F32)


def nn(a, b):
    return lax.dot_general(a, b, (((1,), (0,)), ((), ())), preferred_element_type=F32)


class RingSum:
    def __init__(self, size, me, peer, chunk, sent, landed, send_sem, recv_sem, right):
        self.size, self.me, self.peer, self.chunk = size, me, peer, chunk
        self.sent, self.landed = sent, landed
        self.send_sem, self.recv_sem = send_sem, recv_sem
        self.ways = ((1, right, 0), (-1, size - 1 - right, right))
        self.copies = {}

    def stage(self, step):
        for sign, hops, base in self.ways:
            if step >= hops:
                continue
            slot = base + step
            target = lax.rem(self.me + sign * (hops - step) + self.size, self.size)
            total = self.chunk(target)
            if step > 0:
                self.copies[slot - 1].wait_recv()
                total = total + self.landed(slot - 1)[...].astype(F32)
            self.sent(slot)[...] = total.astype(self.sent(slot).dtype)
            copy = pltpu.make_async_remote_copy(
                src_ref=self.sent(slot),
                dst_ref=self.landed(slot),
                send_sem=self.send_sem(slot),
                recv_sem=self.recv_sem(slot),
                device_id=self.peer(sign),
                device_id_type=MESH,
            )
            copy.start()
            self.copies[slot] = copy

    def final(self):
        total = self.chunk(self.me)
        for _, hops, base in self.ways:
            slot = base + hops - 1
            self.copies[slot].wait_recv()
            total = total + self.landed(slot)[...].astype(F32)
        return total

    def drain(self):
        for copy in self.copies.values():
            copy.wait_send()


class DirectSum:
    def __init__(self, size, me, peer, chunk, sent, landed, send_sem, recv_sem):
        self.size, self.me, self.peer, self.chunk = size, me, peer, chunk
        self.sent, self.landed = sent, landed
        self.send_sem, self.recv_sem = send_sem, recv_sem
        self.copies = []

    def stage(self, step):
        for d in range(1, self.size):
            to = lax.rem(self.me + d, self.size)
            self.sent(d - 1)[...] = self.chunk(to).astype(self.sent(d - 1).dtype)
            copy = pltpu.make_async_remote_copy(
                src_ref=self.sent(d - 1),
                dst_ref=self.landed(d - 1),
                send_sem=self.send_sem(d - 1),
                recv_sem=self.recv_sem(d - 1),
                device_id=self.peer(d),
                device_id_type=MESH,
            )
            copy.start()
            self.copies.append(copy)

    def final(self):
        total = self.chunk(self.me)
        for d, copy in enumerate(self.copies):
            copy.wait_recv()
            total = total + self.landed(d)[...].astype(F32)
        return total

    def drain(self):
        for copy in self.copies:
            copy.wait_send()


def kernel(
    q_hbm,
    g_hbm,
    x_hbm,
    k_hbm,
    v_hbm,
    act_hbm,
    w_hbm,
    len_ref,
    ada_ref,
    own_ref,
    down_ref,
    up_ref,
    qv,
    gv,
    xv,
    kv,
    bias,
    dq,
    wall,
    wz,
    act_v,
    act_cols,
    rank_cols,
    slots,
    pick_y,
    pick_x,
    meta_s,
    meta_r,
    zs,
    zr,
    eb,
    fys,
    fyr,
    fxs,
    fxr,
    sxs,
    sxr,
    sys_,
    syr,
    ty,
    tx,
    load_sem,
    kv_sem,
    wy_sem,
    wx_sem,
    wc_sem,
    wz_sem,
    z_sem,
    e_sem,
    f_sem,
    s_sem,
    m_sem,
):
    s = lax.axis_index("seq")
    z = lax.axis_index("head")
    core = lax.rem(s, 2)
    y = lax.rem(s // 2, NY)
    x = s // (2 * NY)

    def at_z(d):
        return (s, lax.rem(z + d + NZ, NZ))

    def at_y(d):
        return (x * (2 * NY) + lax.rem(y + d + NY, NY) * 2 + core, z)

    def at_x(d):
        return (lax.rem(x + d + NX, NX) * (2 * NY) + y * 2 + core, z)

    partner = (s + 1 - 2 * core, z)

    barrier = pltpu.get_barrier_semaphore()
    others = (
        [at_z(1), at_z(-1), partner]
        + [at_y(d) for d in range(1, NY)]
        + [at_x(d) for d in range(1, NX)]
    )
    for other in others:
        pl.semaphore_signal(barrier, inc=1, device_id=other, device_id_type=MESH)

    places = (core * (NX * NY) + x * NY + y, core * (NX * NY) + y * NX + x)
    load_count = [0]

    def load(src, dst):
        copy = pltpu.make_async_copy(src, dst, load_sem.at[load_count[0]])
        load_count[0] += 1
        copy.start()
        return copy

    own_kv = []
    for g in range(KV_HEADS):
        lanes = pl.ds(g * HEAD_SIZE, HEAD_SIZE)
        own_kv.append([load(src.at[:, lanes], kv.at[HALO, g, i]) for i, src in enumerate((k_hbm, v_hbm))])
    w_load = [load(w_hbm.at[0, :, pl.ds(h * PIECE, PIECE)], wall.at[h, places[h]]) for h in range(2)]
    act_load = load(act_hbm, act_v)

    sends = []

    def remote(src, dst, sem, at, to):
        copy = pltpu.make_async_remote_copy(
            src_ref=src,
            dst_ref=dst,
            send_sem=sem.at[0, at],
            recv_sem=sem.at[1, at],
            device_id=to,
            device_id_type=MESH,
        )
        copy.start()
        sends.append(copy)
        return copy

    kv_copies = {}

    def send_kv(g, d):
        if d == 0:
            for copy in own_kv[g]:
                copy.wait()
        else:
            kv_copies[g, d].wait_recv()
        if d < HALO:
            kv_copies[g, d + 1] = remote(
                kv.at[HALO - d, g], kv.at[HALO - d - 1, g], kv_sem, g * HALO + d, at_z(1)
            )

    for copy in w_load:
        copy.wait()
    pl.semaphore_wait(barrier, len(others))

    def pass_w(h, rows, sem, at, to):
        return remote(wall.at[h, rows], wall.at[h, rows], sem, at, to)

    w_one = [
        [pass_w(0, places[0], wy_sem, d, at_y(d)) for d in range(1, NY)],
        [pass_w(1, places[1], wx_sem, d, at_x(d)) for d in range(1, NX)],
    ]
    for g in range(KV_HEADS):
        send_kv(g, 0)
    qg_load = []
    for g in range(KV_HEADS):
        lanes = pl.ds(g * GROUP * HEAD_SIZE, GROUP * HEAD_SIZE)
        qg_load.append([load(src.at[:, lanes], dst.at[:, lanes]) for src, dst in ((q_hbm, qv), (g_hbm, gv))])

    ends, total = [], 0
    for i in range(SEGMENTS):
        total = total + len_ref[0, i]
        ends.append(total)
    starts = [0] + ends[:-1]
    lane = lax.broadcasted_iota(I32, (8, COLS), 1)
    slot = lax.rem(lane, RANK)
    for i in range(SEGMENTS):
        owner = own_ref[ada_ref[0, i]]
        slot = slot + jnp.where(lane // RANK == i, owner * RANK, 0)
    meta_s[...] = slot
    slots[:, 0:COLS] = slot
    meta = remote(meta_s, meta_r, m_sem, 0, partner)

    first = z * TOKENS
    row_pos = first + lax.broadcasted_iota(I32, (TOKENS, 1), 0)
    row_start = jnp.zeros((TOKENS, 1), I32)
    for i in range(1, SEGMENTS):
        row_start = jnp.where(row_pos >= starts[i], starts[i], row_start)
    key_pos = first - HALO * TOKENS + lax.broadcasted_iota(I32, (TOKENS, KEYS), 1)
    allowed = (key_pos >= row_start) & (key_pos <= row_pos)
    bias[...] = jnp.where(allowed, 0.0, -1e30).astype(F32)

    col = lax.broadcasted_iota(I32, (COLS, 1), 0)
    col_start = jnp.zeros((COLS, 1), I32)
    col_end = jnp.zeros((COLS, 1), I32)
    col_rows = [lax.rem(col, RANK)] * 2
    for i in range(SEGMENTS):
        here = col // RANK == i
        col_start = jnp.where(here, starts[i], col_start)
        col_end = jnp.where(here, ends[i], col_end)
        adapter = ada_ref[0, i]
        chip = adapter // 2
        for h, at in enumerate((chip, lax.rem(chip, NY) * NX + chip // NY)):
            adapter_row = (lax.rem(adapter, 2) * (NX * NY) + at) * RANK
            col_rows[h] = col_rows[h] + jnp.where(here, adapter_row, 0)
    token = first + lax.broadcasted_iota(I32, (COLS, TOKENS), 1)
    mask = (token >= col_start) & (token < col_end)
    spread = lax.rem(lax.broadcasted_iota(I32, (COLS, RANK), 0), RANK) == lax.broadcasted_iota(
        I32, (COLS, RANK), 1
    )
    spread = jnp.where(spread, 1.0, 0.0).astype(BF16)
    act_load.wait()
    act_cols[...] = jnp.where(mask, nn(spread, act_v[...]), 0.0).astype(BF16)

    def attend(g):
        for copy in qg_load[g]:
            copy.wait()
        kv_copies[g, HALO].wait_recv()

        def heads(i, carry):
            at = [
                pl.ds(pl.multiple_of((g * GROUP + PAIR * i + j) * HEAD_SIZE, HEAD_SIZE), HEAD_SIZE)
                for j in range(PAIR)
            ]
            keys = kv[:, g, 0].reshape(KEYS, HEAD_SIZE)
            values = kv[:, g, 1].reshape(KEYS, HEAD_SIZE)
            q_rows = jnp.concatenate([qv[:, lanes] for lanes in at], axis=0)
            g_rows = jnp.concatenate([gv[:, lanes] for lanes in at], axis=0)
            hidden = jnp.concatenate([bias[...]] * PAIR, axis=0)
            scores = nt(q_rows, keys) * SCORE_SCALE + hidden
            weights = jnp.exp(scores - jnp.max(scores, axis=1, keepdims=True))
            scale = 1.0 / jnp.sum(weights, axis=1, keepdims=True)
            d_prob = nt(g_rows, values)
            delta = jnp.sum(weights * d_prob, axis=1, keepdims=True) * scale
            dscore = (weights * (d_prob - delta) * (scale * SCORE_SCALE)).astype(BF16)
            grads = nn(dscore, keys).astype(BF16)
            for j in range(PAIR):
                dq[:, at[j]] = grads[j * TOKENS : (j + 1) * TOKENS]
            return carry

        lax.fori_loop(0, GROUP // PAIR, heads, 0)

    mine = core * (NX * NY)
    for copy in w_one[1]:
        copy.wait_recv()
    row = pl.ds(mine + y * NX, NX)
    w_two = [None, [pass_w(1, row, wy_sem, NY + d, at_y(d)) for d in range(1, NY)]]
    for copy in w_one[0]:
        copy.wait_recv()
    row = pl.ds(mine + x * NY, NY)
    w_two[0] = [pass_w(0, row, wx_sem, NX + d, at_x(d)) for d in range(1, NX)]
    for g in range(KV_HEADS):
        send_kv(g, 1)
    w_core = []
    for h in range(2):
        for copy in w_two[h]:
            copy.wait_recv()
        w_core.append(pass_w(h, pl.ds(mine, NX * NY), wc_sem, h, partner))
    for g in range(KV_HEADS):
        send_kv(g, 2)
    x_load = load(x_hbm, xv)
    meta.wait_recv()
    slots[:, COLS : 2 * COLS] = meta_r[...]

    wz_ways = ((1, 3, 0), (-1, 4, 3))
    wz_copies = {}

    def pass_on(h, step):
        for sign, hops, base in wz_ways:
            if step <= hops:
                if step > 0:
                    wz_copies[h, base + step - 1].wait_recv()
                if step < hops:
                    at = lax.rem(z - sign * step + NZ, NZ)
                    wz_copies[h, base + step] = remote(
                        wz.at[at, h], wz.at[at, h], wz_sem, h * (NZ - 1) + base + step, at_z(sign)
                    )

    every = lax.broadcasted_iota(I32, (COLS, 2 * NX * NY * RANK), 1)
    for h in range(2):
        w_core[h].wait_recv()
        pick = jnp.where(every == col_rows[h], 1.0, 0.0).astype(BF16)
        wz[z, h] = nn(pick, wall[h].reshape(2 * NX * NY * RANK, PIECE)).astype(BF16)
        pass_on(h, 0)
    def fill(i, carry):
        row = i * (NX * RANK) + lax.broadcasted_iota(I32, (NX * RANK, 2 * COLS), 0)
        low = core * RANK + lax.rem(row, RANK)
        chip = row // RANK
        rows = pl.ds(pl.multiple_of(i * (NX * RANK), NX * RANK), NX * RANK)
        key = (lax.rem(chip, NX) * NY + chip // NX) * (2 * RANK) + low
        pick_y[rows, :] = jnp.where(key == slots[0:1, :], 1.0, 0.0).astype(BF16)
        pick_x[rows, :] = jnp.where(chip * (2 * RANK) + low == slots[0:1, :], 1.0, 0.0).astype(BF16)
        return carry

    lax.fori_loop(0, NY, fill, 0)
    for g in range(KV_HEADS):
        attend(g)
        if g < 3:
            for h in range(2):
                pass_on(h, g + 1)

    def zcols(ref, c, i, width):
        return ref[:, pl.ds(pl.multiple_of(c * width + i * PIECE, PIECE), PIECE)]

    def z_chunk(p, c):
        if p < 2:
            return nn(act_cols[...], zcols(dq, c, p, WIDTH))
        return nn(rank_cols[...], zcols(xv, c, p - 2, 2 * WIDTH))

    def y_chunk(p, c):
        rows = pl.ds(pl.multiple_of(c * (NX * RANK), NX * RANK), NX * RANK)
        return nn(pick_y[rows, :], eb[p])

    def x_chunk(p, c):
        rows = pl.ds(pl.multiple_of(c * (NY * RANK), NY * RANK), NY * RANK)
        return nn(pick_x[rows, :], eb[p])

    def rows_of(buf, c):
        return buf[pl.ds(pl.multiple_of(c * RANK, RANK), RANK), :]

    def refs(p, at, sent, landed, sem):
        return (
            lambda i: sent.at[at, i],
            lambda i: landed.at[at, i],
            lambda i: sem.at[0, p, i],
            lambda i: sem.at[1, p, i],
        )

    z_sums, f_sums, s_sums, held, e_copies = [], [], [], [], {}
    for p in range(PIECES):
        z_sums.append(
            RingSum(NZ, z, at_z, functools.partial(z_chunk, p), *refs(p, p, zs, zr, z_sem), 4 - p % 2)
        )
        at = sum((i in Y_FIRST) == (p in Y_FIRST) for i in range(p))
        if p in Y_FIRST:
            held.append(ty.at[at])
            f_sums.append(
                DirectSum(NY, y, at_y, functools.partial(y_chunk, p), *refs(p, at, fys, fyr, f_sem))
            )
            s_sums.append(
                DirectSum(NX, x, at_x, functools.partial(rows_of, ty.at[at]), *refs(p, at, sxs, sxr, s_sem))
            )
        else:
            held.append(tx.at[at])
            f_sums.append(
                RingSum(NX, x, at_x, functools.partial(x_chunk, p), *refs(p, at, fxs, fxr, f_sem), 1 + p % 2)
            )
            s_sums.append(
                DirectSum(NY, y, at_y, functools.partial(rows_of, tx.at[at]), *refs(p, at, sys_, syr, s_sem))
            )

    def to_partner(p):
        eb[p, 0:COLS] = z_sums[p].final().astype(BF16)
        e_copies[p] = remote(eb.at[p, pl.ds(0, COLS)], eb.at[p, pl.ds(COLS, COLS)], e_sem, p, partner)

    def first_hop(p):
        e_copies[p].wait_recv()
        f_sums[p].stage(0)

    def turn(p):
        held[p][...] = f_sums[p].final()
        s_sums[p].stage(0)

    def write(p):
        ref, at = (up_ref, p) if p < 2 else (down_ref, p - 2)
        ref[:, at * PIECE : (at + 1) * PIECE] = s_sums[p].final() * ADAPTER_SCALE

    def rank_all():
        for h in range(2):
            pass_on(h, 4)
        rank = jnp.zeros((COLS, TOKENS), F32)
        for c in range(NZ):
            for h in range(2):
                at = c * WIDTH + h * PIECE
                rank = rank + nt(wz[c, h], dq[:, at : at + PIECE])
        rank_cols[...] = jnp.where(mask, rank, 0.0).astype(BF16)
        x_load.wait()

    plan = []
    for p, begin in enumerate(BEGIN):
        steps = [functools.partial(z_sums[p].stage, i) for i in range(4)]
        steps += [functools.partial(to_partner, p), functools.partial(first_hop, p)]
        if p not in Y_FIRST:
            steps.append(functools.partial(f_sums[p].stage, 1))
        steps += [functools.partial(turn, p), functools.partial(write, p)]
        plan += [(begin + i, 0 if i < 5 else 1, p, step) for i, step in enumerate(steps)]
    plan.append((0, -1, 0, rank_all))
    for _, _, _, step in sorted(plan, key=lambda entry: entry[:3]):
        step()

    for copy in sends:
        copy.wait_send()
    for sums in z_sums + f_sums + s_sums:
        sums.drain()


def on_device(q, k, v, g, x, act, w, length, adapter, owner):
    vmem = pl.BlockSpec(memory_space=pltpu.VMEM)
    smem = pl.BlockSpec(memory_space=pltpu.SMEM)
    hbm = pl.BlockSpec(memory_space=pl.ANY)
    dma = pltpu.SemaphoreType.DMA
    ring = NZ - 1
    by_y = len(Y_FIRST)
    by_x = PIECES - by_y
    features = KV_HEADS * GROUP * HEAD_SIZE
    scratch = [
        pltpu.VMEM((TOKENS, features), BF16),
        pltpu.VMEM((TOKENS, features), BF16),
        pltpu.VMEM((TOKENS, x.shape[1]), BF16),
        pltpu.VMEM((HALO + 1, KV_HEADS, 2, TOKENS, HEAD_SIZE), BF16),
        pltpu.VMEM((TOKENS, KEYS), F32),
        pltpu.VMEM((TOKENS, features), BF16),
        pltpu.VMEM((2, 2 * NX * NY, RANK, PIECE), BF16),
        pltpu.VMEM((NZ, 2, COLS, PIECE), BF16),
        pltpu.VMEM((RANK, TOKENS), BF16),
        pltpu.VMEM((COLS, TOKENS), BF16),
        pltpu.VMEM((COLS, TOKENS), BF16),
        pltpu.VMEM((8, 2 * COLS), I32),
        pltpu.VMEM((NX * NY * RANK, 2 * COLS), BF16),
        pltpu.VMEM((NX * NY * RANK, 2 * COLS), BF16),
        pltpu.VMEM((8, COLS), I32),
        pltpu.VMEM((8, COLS), I32),
        pltpu.VMEM((PIECES, ring, COLS, PIECE), BF16),
        pltpu.VMEM((PIECES, ring, COLS, PIECE), BF16),
        pltpu.VMEM((PIECES, 2 * COLS, PIECE), BF16),
        pltpu.VMEM((by_y, NY - 1, NX * RANK, PIECE), BF16),
        pltpu.VMEM((by_y, NY - 1, NX * RANK, PIECE), BF16),
        pltpu.VMEM((by_x, NX - 1, NY * RANK, PIECE), BF16),
        pltpu.VMEM((by_x, NX - 1, NY * RANK, PIECE), BF16),
        pltpu.VMEM((by_y, NX - 1, RANK, PIECE), BF16),
        pltpu.VMEM((by_y, NX - 1, RANK, PIECE), BF16),
        pltpu.VMEM((by_x, NY - 1, RANK, PIECE), BF16),
        pltpu.VMEM((by_x, NY - 1, RANK, PIECE), BF16),
        pltpu.VMEM((by_y, NX * RANK, PIECE), F32),
        pltpu.VMEM((by_x, NY * RANK, PIECE), F32),
        dma((4 * KV_HEADS + 4,)),
        dma((2, KV_HEADS * HALO)),
        dma((2, 2 * NY)),
        dma((2, 2 * NX)),
        dma((2, 2)),
        dma((2, 2 * ring)),
        dma((2, PIECES, ring)),
        dma((2, PIECES)),
        dma((2, PIECES, ring)),
        dma((2, PIECES, ring)),
        dma((2, 1)),
    ]
    down, up = pl.pallas_call(
        kernel,
        out_shape=(
            jax.ShapeDtypeStruct((RANK, 2 * WIDTH), F32),
            jax.ShapeDtypeStruct((RANK, WIDTH), F32),
        ),
        in_specs=[hbm] * 7 + [smem] * 3,
        out_specs=(vmem, vmem),
        scratch_shapes=scratch,
        compiler_params=pltpu.CompilerParams(
            collective_id=0, has_side_effects=True, vmem_limit_bytes=60 * 1024 * 1024
        ),
    )(q, g, x, k, v, act.T, w, length, adapter, owner)
    return down.T[None], up[None]


def solution(mesh):
    return jax.shard_map(
        on_device,
        mesh=mesh,
        in_specs=(
            P(("seq", "head"), None),
            P(("seq", "head"), None),
            P(("seq", "head"), None),
            P(("seq", "head"), None),
            P(("seq", "head"), None),
            P(("seq", "head"), None),
            P("seq", None, "head"),
            P("seq", None),
            P("seq", None),
            P(),
        ),
        out_specs=(P("seq", "head", None), P("seq", None, "head")),
        check_vma=False,
    )
```

```python
import functools

import jax
import jax.numpy as jnp
from jax import lax
from jax.experimental import pallas as pl
from jax.experimental.pallas import tpu as pltpu
from jax.sharding import PartitionSpec as P

MESH = pl.DeviceIdType.MESH
F32, BF16, I32 = jnp.float32, jnp.bfloat16, jnp.int32

NX, NY, NZ = 4, 8, 8
HEAD_SIZE = 128
KV_HEADS = 4
GROUP = 8
RANK = 16
PAIR = 2
SEGMENTS = 8
COLS = SEGMENTS * RANK
TOKENS = 128
HALO = 3
KEYS = (HALO + 1) * TOKENS
WIDTH = 512
PIECE = 256
PIECES = 6
BEGIN = (-1, -1, 0, 0, 1, 1)
Y_FIRST = (0, 2, 4)
ADAPTER_SCALE = 2.0
SCORE_SCALE = 1.0 / HEAD_SIZE**0.5


def nt(a, b):
    return lax.dot_general(a, b, (((1,), (1,)), ((), ())), preferred_element_type=F32)


def nn(a, b):
    return lax.dot_general(a, b, (((1,), (0,)), ((), ())), preferred_element_type=F32)


class RingSum:
    def __init__(self, size, me, peer, chunk, sent, landed, send_sem, recv_sem, right):
        self.size, self.me, self.peer, self.chunk = size, me, peer, chunk
        self.sent, self.landed = sent, landed
        self.send_sem, self.recv_sem = send_sem, recv_sem
        self.ways = ((1, right, 0), (-1, size - 1 - right, right))
        self.copies = {}

    def stage(self, step):
        for sign, hops, base in self.ways:
            if step >= hops:
                continue
            slot = base + step
            target = lax.rem(self.me + sign * (hops - step) + self.size, self.size)
            total = self.chunk(target)
            if step > 0:
                self.copies[slot - 1].wait_recv()
                total = total + self.landed(slot - 1)[...].astype(F32)
            self.sent(slot)[...] = total.astype(self.sent(slot).dtype)
            copy = pltpu.make_async_remote_copy(
                src_ref=self.sent(slot),
                dst_ref=self.landed(slot),
                send_sem=self.send_sem(slot),
                recv_sem=self.recv_sem(slot),
                device_id=self.peer(sign),
                device_id_type=MESH,
            )
            copy.start()
            self.copies[slot] = copy

    def final(self):
        total = self.chunk(self.me)
        for _, hops, base in self.ways:
            slot = base + hops - 1
            self.copies[slot].wait_recv()
            total = total + self.landed(slot)[...].astype(F32)
        return total

    def drain(self):
        for copy in self.copies.values():
            copy.wait_send()


class DirectSum:
    def __init__(self, size, me, peer, chunk, sent, landed, send_sem, recv_sem):
        self.size, self.me, self.peer, self.chunk = size, me, peer, chunk
        self.sent, self.landed = sent, landed
        self.send_sem, self.recv_sem = send_sem, recv_sem
        self.copies = []

    def stage(self, step):
        for d in range(1, self.size):
            to = lax.rem(self.me + d, self.size)
            self.sent(d - 1)[...] = self.chunk(to).astype(self.sent(d - 1).dtype)
            copy = pltpu.make_async_remote_copy(
                src_ref=self.sent(d - 1),
                dst_ref=self.landed(d - 1),
                send_sem=self.send_sem(d - 1),
                recv_sem=self.recv_sem(d - 1),
                device_id=self.peer(d),
                device_id_type=MESH,
            )
            copy.start()
            self.copies.append(copy)

    def final(self):
        total = self.chunk(self.me)
        for d, copy in enumerate(self.copies):
            copy.wait_recv()
            total = total + self.landed(d)[...].astype(F32)
        return total

    def drain(self):
        for copy in self.copies:
            copy.wait_send()


def kernel(
    q_hbm,
    g_hbm,
    x_hbm,
    k_hbm,
    v_hbm,
    act_hbm,
    w_hbm,
    len_ref,
    ada_ref,
    own_ref,
    down_ref,
    up_ref,
    qv,
    gv,
    xv,
    kv,
    bias,
    dq,
    wall,
    wz,
    act_v,
    act_cols,
    rank_cols,
    slots,
    pick_y,
    pick_x,
    meta_s,
    meta_r,
    zs,
    zr,
    eb,
    fys,
    fyr,
    fxs,
    fxr,
    sxs,
    sxr,
    sys_,
    syr,
    ty,
    tx,
    load_sem,
    kv_sem,
    wy_sem,
    wx_sem,
    wc_sem,
    wz_sem,
    z_sem,
    e_sem,
    f_sem,
    s_sem,
    m_sem,
):
    s = lax.axis_index("seq")
    z = lax.axis_index("head")
    core = lax.rem(s, 2)
    y = lax.rem(s // 2, NY)
    x = s // (2 * NY)

    def at_z(d):
        return (s, lax.rem(z + d + NZ, NZ))

    def at_y(d):
        return (x * (2 * NY) + lax.rem(y + d + NY, NY) * 2 + core, z)

    def at_x(d):
        return (lax.rem(x + d + NX, NX) * (2 * NY) + y * 2 + core, z)

    partner = (s + 1 - 2 * core, z)

    barrier = pltpu.get_barrier_semaphore()
    others = (
        [at_z(1), at_z(-1), partner]
        + [at_y(d) for d in range(1, NY)]
        + [at_x(d) for d in range(1, NX)]
    )
    for other in others:
        pl.semaphore_signal(barrier, inc=1, device_id=other, device_id_type=MESH)

    places = (core * (NX * NY) + x * NY + y, core * (NX * NY) + y * NX + x)
    load_count = [0]

    def load(src, dst):
        copy = pltpu.make_async_copy(src, dst, load_sem.at[load_count[0]])
        load_count[0] += 1
        copy.start()
        return copy

    own_kv = []
    for g in range(KV_HEADS):
        lanes = pl.ds(g * HEAD_SIZE, HEAD_SIZE)
        own_kv.append([load(src.at[:, lanes], kv.at[HALO, g, i]) for i, src in enumerate((k_hbm, v_hbm))])
    w_load = [load(w_hbm.at[0, :, pl.ds(h * PIECE, PIECE)], wall.at[h, places[h]]) for h in range(2)]
    act_load = load(act_hbm, act_v)
    qg_load = []
    for g in range(KV_HEADS):
        lanes = pl.ds(g * GROUP * HEAD_SIZE, GROUP * HEAD_SIZE)
        qg_load.append([load(src.at[:, lanes], dst.at[:, lanes]) for src, dst in ((q_hbm, qv), (g_hbm, gv))])

    sends = []

    def remote(src, dst, sem, at, to):
        copy = pltpu.make_async_remote_copy(
            src_ref=src,
            dst_ref=dst,
            send_sem=sem.at[0, at],
            recv_sem=sem.at[1, at],
            device_id=to,
            device_id_type=MESH,
        )
        copy.start()
        sends.append(copy)
        return copy

    kv_copies = {}

    def send_kv(g, d):
        if d == 0:
            for copy in own_kv[g]:
                copy.wait()
        else:
            kv_copies[g, d].wait_recv()
        if d < HALO:
            kv_copies[g, d + 1] = remote(
                kv.at[HALO - d, g], kv.at[HALO - d - 1, g], kv_sem, g * HALO + d, at_z(1)
            )

    for copy in w_load:
        copy.wait()
    pl.semaphore_wait(barrier, len(others))

    def pass_w(h, rows, sem, at, to):
        return remote(wall.at[h, rows], wall.at[h, rows], sem, at, to)

    w_one = [
        [pass_w(0, places[0], wy_sem, d, at_y(d)) for d in range(1, NY)],
        [pass_w(1, places[1], wx_sem, d, at_x(d)) for d in range(1, NX)],
    ]
    send_kv(0, 0)
    send_kv(1, 0)

    ends, total = [], 0
    for i in range(SEGMENTS):
        total = total + len_ref[0, i]
        ends.append(total)
    starts = [0] + ends[:-1]
    lane = lax.broadcasted_iota(I32, (8, COLS), 1)
    slot = lax.rem(lane, RANK)
    for i in range(SEGMENTS):
        owner = own_ref[ada_ref[0, i]]
        slot = slot + jnp.where(lane // RANK == i, owner * RANK, 0)
    meta_s[...] = slot
    slots[:, 0:COLS] = slot
    meta = remote(meta_s, meta_r, m_sem, 0, partner)

    first = z * TOKENS
    row_pos = first + lax.broadcasted_iota(I32, (TOKENS, 1), 0)
    row_start = jnp.zeros((TOKENS, 1), I32)
    for i in range(1, SEGMENTS):
        row_start = jnp.where(row_pos >= starts[i], starts[i], row_start)
    key_pos = first - HALO * TOKENS + lax.broadcasted_iota(I32, (TOKENS, KEYS), 1)
    allowed = (key_pos >= row_start) & (key_pos <= row_pos)
    bias[...] = jnp.where(allowed, 0.0, -1e30).astype(F32)

    col = lax.broadcasted_iota(I32, (COLS, 1), 0)
    col_start = jnp.zeros((COLS, 1), I32)
    col_end = jnp.zeros((COLS, 1), I32)
    col_rows = [lax.rem(col, RANK)] * 2
    for i in range(SEGMENTS):
        here = col // RANK == i
        col_start = jnp.where(here, starts[i], col_start)
        col_end = jnp.where(here, ends[i], col_end)
        adapter = ada_ref[0, i]
        chip = adapter // 2
        for h, at in enumerate((chip, lax.rem(chip, NY) * NX + chip // NY)):
            adapter_row = (lax.rem(adapter, 2) * (NX * NY) + at) * RANK
            col_rows[h] = col_rows[h] + jnp.where(here, adapter_row, 0)
    token = first + lax.broadcasted_iota(I32, (COLS, TOKENS), 1)
    mask = (token >= col_start) & (token < col_end)
    spread = lax.rem(lax.broadcasted_iota(I32, (COLS, RANK), 0), RANK) == lax.broadcasted_iota(
        I32, (COLS, RANK), 1
    )
    spread = jnp.where(spread, 1.0, 0.0).astype(BF16)
    act_load.wait()
    act_cols[...] = jnp.where(mask, nn(spread, act_v[...]), 0.0).astype(BF16)

    def attend(g):
        for copy in qg_load[g]:
            copy.wait()
        kv_copies[g, HALO].wait_recv()

        def heads(i, carry):
            at = [
                pl.ds(pl.multiple_of((g * GROUP + PAIR * i + j) * HEAD_SIZE, HEAD_SIZE), HEAD_SIZE)
                for j in range(PAIR)
            ]
            keys = kv[:, g, 0].reshape(KEYS, HEAD_SIZE)
            values = kv[:, g, 1].reshape(KEYS, HEAD_SIZE)
            q_rows = jnp.concatenate([qv[:, lanes] for lanes in at], axis=0)
            g_rows = jnp.concatenate([gv[:, lanes] for lanes in at], axis=0)
            hidden = jnp.concatenate([bias[...]] * PAIR, axis=0)
            scores = nt(q_rows, keys) * SCORE_SCALE + hidden
            weights = jnp.exp(scores - jnp.max(scores, axis=1, keepdims=True))
            scale = 1.0 / jnp.sum(weights, axis=1, keepdims=True)
            d_prob = nt(g_rows, values)
            delta = jnp.sum(weights * d_prob, axis=1, keepdims=True) * scale
            dscore = (weights * (d_prob - delta) * (scale * SCORE_SCALE)).astype(BF16)
            grads = nn(dscore, keys).astype(BF16)
            for j in range(PAIR):
                dq[:, at[j]] = grads[j * TOKENS : (j + 1) * TOKENS]
            return carry

        lax.fori_loop(0, GROUP // PAIR, heads, 0)

    mine = core * (NX * NY)
    for copy in w_one[1]:
        copy.wait_recv()
    row = pl.ds(mine + y * NX, NX)
    w_two = [None, [pass_w(1, row, wy_sem, NY + d, at_y(d)) for d in range(1, NY)]]
    send_kv(0, 1)
    send_kv(2, 0)
    for copy in w_one[0]:
        copy.wait_recv()
    row = pl.ds(mine + x * NY, NY)
    w_two[0] = [pass_w(0, row, wx_sem, NX + d, at_x(d)) for d in range(1, NX)]
    for g, d in ((1, 1), (3, 0), (0, 2), (2, 1), (1, 2)):
        send_kv(g, d)
    meta.wait_recv()
    slots[:, COLS : 2 * COLS] = meta_r[...]
    w_core = []
    for h in range(2):
        for copy in w_two[h]:
            copy.wait_recv()
        w_core.append(pass_w(h, pl.ds(mine, NX * NY), wc_sem, h, partner))
    send_kv(3, 1)
    send_kv(2, 2)

    wz_ways = ((1, 3, 0), (-1, 4, 3))
    wz_copies = {}

    def pass_on(h, step):
        for sign, hops, base in wz_ways:
            if step <= hops:
                if step > 0:
                    wz_copies[h, base + step - 1].wait_recv()
                if step < hops:
                    at = lax.rem(z - sign * step + NZ, NZ)
                    wz_copies[h, base + step] = remote(
                        wz.at[at, h], wz.at[at, h], wz_sem, h * (NZ - 1) + base + step, at_z(sign)
                    )

    attend(0)
    send_kv(3, 2)
    every = lax.broadcasted_iota(I32, (COLS, 2 * NX * NY * RANK), 1)
    for h in range(2):
        w_core[h].wait_recv()
        pick = jnp.where(every == col_rows[h], 1.0, 0.0).astype(BF16)
        wz[z, h] = nn(pick, wall[h].reshape(2 * NX * NY * RANK, PIECE)).astype(BF16)
        pass_on(h, 0)
    x_load = load(x_hbm, xv)

    def fill(i, carry):
        row = i * (NX * RANK) + lax.broadcasted_iota(I32, (NX * RANK, 2 * COLS), 0)
        low = core * RANK + lax.rem(row, RANK)
        chip = row // RANK
        rows = pl.ds(pl.multiple_of(i * (NX * RANK), NX * RANK), NX * RANK)
        key = (lax.rem(chip, NX) * NY + chip // NX) * (2 * RANK) + low
        pick_y[rows, :] = jnp.where(key == slots[0:1, :], 1.0, 0.0).astype(BF16)
        pick_x[rows, :] = jnp.where(chip * (2 * RANK) + low == slots[0:1, :], 1.0, 0.0).astype(BF16)
        return carry

    lax.fori_loop(0, NY, fill, 0)
    for g in range(1, KV_HEADS):
        attend(g)
        for h in range(2):
            pass_on(h, g)

    def zcols(ref, c, i, width):
        return ref[:, pl.ds(pl.multiple_of(c * width + i * PIECE, PIECE), PIECE)]

    def z_chunk(p, c):
        if p < 2:
            return nn(act_cols[...], zcols(dq, c, p, WIDTH))
        return nn(rank_cols[...], zcols(xv, c, p - 2, 2 * WIDTH))

    def y_chunk(p, c):
        rows = pl.ds(pl.multiple_of(c * (NX * RANK), NX * RANK), NX * RANK)
        return nn(pick_y[rows, :], eb[p])

    def x_chunk(p, c):
        rows = pl.ds(pl.multiple_of(c * (NY * RANK), NY * RANK), NY * RANK)
        return nn(pick_x[rows, :], eb[p])

    def rows_of(buf, c):
        return buf[pl.ds(pl.multiple_of(c * RANK, RANK), RANK), :]

    def refs(p, at, sent, landed, sem):
        return (
            lambda i: sent.at[at, i],
            lambda i: landed.at[at, i],
            lambda i: sem.at[0, p, i],
            lambda i: sem.at[1, p, i],
        )

    z_sums, f_sums, s_sums, held, e_copies = [], [], [], [], {}
    for p in range(PIECES):
        z_sums.append(
            RingSum(NZ, z, at_z, functools.partial(z_chunk, p), *refs(p, p, zs, zr, z_sem), 4 - p % 2)
        )
        at = sum((i in Y_FIRST) == (p in Y_FIRST) for i in range(p))
        if p in Y_FIRST:
            held.append(ty.at[at])
            f_sums.append(
                DirectSum(NY, y, at_y, functools.partial(y_chunk, p), *refs(p, at, fys, fyr, f_sem))
            )
            s_sums.append(
                DirectSum(NX, x, at_x, functools.partial(rows_of, ty.at[at]), *refs(p, at, sxs, sxr, s_sem))
            )
        else:
            held.append(tx.at[at])
            f_sums.append(
                DirectSum(NX, x, at_x, functools.partial(x_chunk, p), *refs(p, at, fxs, fxr, f_sem))
            )
            s_sums.append(
                DirectSum(NY, y, at_y, functools.partial(rows_of, tx.at[at]), *refs(p, at, sys_, syr, s_sem))
            )

    def to_partner(p):
        eb[p, 0:COLS] = z_sums[p].final().astype(BF16)
        e_copies[p] = remote(eb.at[p, pl.ds(0, COLS)], eb.at[p, pl.ds(COLS, COLS)], e_sem, p, partner)

    def first_hop(p):
        e_copies[p].wait_recv()
        f_sums[p].stage(0)

    def turn(p):
        held[p][...] = f_sums[p].final()
        s_sums[p].stage(0)

    def write(p):
        ref, at = (up_ref, p) if p < 2 else (down_ref, p - 2)
        ref[:, at * PIECE : (at + 1) * PIECE] = s_sums[p].final() * ADAPTER_SCALE

    def rank_all():
        rank = jnp.zeros((COLS, TOKENS), F32)
        for d in (0, -1, 1, -2, 2, -3, 3, 4):
            c = lax.rem(z + d + NZ, NZ)
            for h in range(2):
                if d == 4:
                    pass_on(h, 4)
                rank = rank + nt(wz[c, h], zcols(dq, c, h, WIDTH))
        rank_cols[...] = jnp.where(mask, rank, 0.0).astype(BF16)
        x_load.wait()

    plan = []
    for p, begin in enumerate(BEGIN):
        steps = [functools.partial(z_sums[p].stage, i) for i in range(4)]
        steps += [functools.partial(to_partner, p), functools.partial(first_hop, p)]
        steps += [functools.partial(turn, p), functools.partial(write, p)]
        late = (1, 2, 2) if begin == 0 else (1, 1, 1)
        when = [(begin + i, (0.5 if begin < 0 else 0, 0 if begin >= 0 else 0.5, 0 if begin >= 0 else 0.5, 0 if begin >= 0 else 0.5, 2, *late)[i]) for i in range(8)]
        if begin < 0:
            when[6:] = [(6, 3), (8, 0)]
        plan += [(*at, p, step) for at, step in zip(when, steps)]
    plan.append((0, -1, 0, rank_all))
    for _, _, _, step in sorted(plan, key=lambda entry: entry[:3]):
        step()

    for copy in sends:
        copy.wait_send()
    for sums in z_sums + f_sums + s_sums:
        sums.drain()


def on_device(q, k, v, g, x, act, w, length, adapter, owner):
    vmem = pl.BlockSpec(memory_space=pltpu.VMEM)
    smem = pl.BlockSpec(memory_space=pltpu.SMEM)
    hbm = pl.BlockSpec(memory_space=pl.ANY)
    dma = pltpu.SemaphoreType.DMA
    ring = NZ - 1
    by_y = len(Y_FIRST)
    by_x = PIECES - by_y
    features = KV_HEADS * GROUP * HEAD_SIZE
    scratch = [
        pltpu.VMEM((TOKENS, features), BF16),
        pltpu.VMEM((TOKENS, features), BF16),
        pltpu.VMEM((TOKENS, x.shape[1]), BF16),
        pltpu.VMEM((HALO + 1, KV_HEADS, 2, TOKENS, HEAD_SIZE), BF16),
        pltpu.VMEM((TOKENS, KEYS), F32),
        pltpu.VMEM((TOKENS, features), BF16),
        pltpu.VMEM((2, 2 * NX * NY, RANK, PIECE), BF16),
        pltpu.VMEM((NZ, 2, COLS, PIECE), BF16),
        pltpu.VMEM((RANK, TOKENS), BF16),
        pltpu.VMEM((COLS, TOKENS), BF16),
        pltpu.VMEM((COLS, TOKENS), BF16),
        pltpu.VMEM((8, 2 * COLS), I32),
        pltpu.VMEM((NX * NY * RANK, 2 * COLS), BF16),
        pltpu.VMEM((NX * NY * RANK, 2 * COLS), BF16),
        pltpu.VMEM((8, COLS), I32),
        pltpu.VMEM((8, COLS), I32),
        pltpu.VMEM((PIECES, ring, COLS, PIECE), BF16),
        pltpu.VMEM((PIECES, ring, COLS, PIECE), BF16),
        pltpu.VMEM((PIECES, 2 * COLS, PIECE), BF16),
        pltpu.VMEM((by_y, NY - 1, NX * RANK, PIECE), BF16),
        pltpu.VMEM((by_y, NY - 1, NX * RANK, PIECE), BF16),
        pltpu.VMEM((by_x, NX - 1, NY * RANK, PIECE), BF16),
        pltpu.VMEM((by_x, NX - 1, NY * RANK, PIECE), BF16),
        pltpu.VMEM((by_y, NX - 1, RANK, PIECE), BF16),
        pltpu.VMEM((by_y, NX - 1, RANK, PIECE), BF16),
        pltpu.VMEM((by_x, NY - 1, RANK, PIECE), BF16),
        pltpu.VMEM((by_x, NY - 1, RANK, PIECE), BF16),
        pltpu.VMEM((by_y, NX * RANK, PIECE), F32),
        pltpu.VMEM((by_x, NY * RANK, PIECE), F32),
        dma((4 * KV_HEADS + 4,)),
        dma((2, KV_HEADS * HALO)),
        dma((2, 2 * NY)),
        dma((2, 2 * NX)),
        dma((2, 2)),
        dma((2, 2 * ring)),
        dma((2, PIECES, ring)),
        dma((2, PIECES)),
        dma((2, PIECES, ring)),
        dma((2, PIECES, ring)),
        dma((2, 1)),
    ]
    down, up = pl.pallas_call(
        kernel,
        out_shape=(
            jax.ShapeDtypeStruct((RANK, 2 * WIDTH), F32),
            jax.ShapeDtypeStruct((RANK, WIDTH), F32),
        ),
        in_specs=[hbm] * 7 + [smem] * 3,
        out_specs=(vmem, vmem),
        scratch_shapes=scratch,
        compiler_params=pltpu.CompilerParams(
            collective_id=0, has_side_effects=True, vmem_limit_bytes=60 * 1024 * 1024
        ),
    )(q, g, x, k, v, act.T, w, length, adapter, owner)
    return down.T[None], up[None]


def solution(mesh):
    return jax.shard_map(
        on_device,
        mesh=mesh,
        in_specs=(
            P(("seq", "head"), None),
            P(("seq", "head"), None),
            P(("seq", "head"), None),
            P(("seq", "head"), None),
            P(("seq", "head"), None),
            P(("seq", "head"), None),
            P("seq", None, "head"),
            P("seq", None),
            P("seq", None),
            P(),
        ),
        out_specs=(P("seq", "head", None), P("seq", None, "head")),
        check_vma=False,
    )
```

```python
import functools

import jax
import jax.numpy as jnp
from jax import lax
from jax.experimental import pallas as pl
from jax.experimental.pallas import tpu as pltpu
from jax.sharding import PartitionSpec as P

MESH = pl.DeviceIdType.MESH
F32, BF16, I32 = jnp.float32, jnp.bfloat16, jnp.int32

NX, NY, NZ = 4, 8, 8
HEAD_SIZE = 128
KV_HEADS = 4
GROUP = 8
RANK = 16
PAIR = 2
FAR = 2
SEGMENTS = 8
COLS = SEGMENTS * RANK
TOKENS = 128
HALO = 3
KEYS = (HALO + 1) * TOKENS
WIDTH = 512
PIECE = 256
PIECES = 6
BEGIN = (-2, -2, 0, 0, 1, 1)
Y_FIRST = (0, 2, 4)
ADAPTER_SCALE = 2.0
SCORE_SCALE = 1.0 / HEAD_SIZE**0.5


def nt(a, b):
    return lax.dot_general(a, b, (((1,), (1,)), ((), ())), preferred_element_type=F32)


def nn(a, b):
    return lax.dot_general(a, b, (((1,), (0,)), ((), ())), preferred_element_type=F32)


class RingSum:
    def __init__(self, size, me, peer, chunk, sent, landed, send_sem, recv_sem, right):
        self.size, self.me, self.peer, self.chunk = size, me, peer, chunk
        self.sent, self.landed = sent, landed
        self.send_sem, self.recv_sem = send_sem, recv_sem
        self.ways = ((1, right, 0), (-1, size - 1 - right, right))
        self.copies = {}

    def stage(self, step):
        for sign, hops, base in self.ways:
            if step >= hops:
                continue
            slot = base + step
            target = lax.rem(self.me + sign * (hops - step) + self.size, self.size)
            total = self.chunk(target)
            if step > 0:
                self.copies[slot - 1].wait_recv()
                total = total + self.landed(slot - 1)[...].astype(F32)
            self.sent(slot)[...] = total.astype(self.sent(slot).dtype)
            copy = pltpu.make_async_remote_copy(
                src_ref=self.sent(slot),
                dst_ref=self.landed(slot),
                send_sem=self.send_sem(slot),
                recv_sem=self.recv_sem(slot),
                device_id=self.peer(sign),
                device_id_type=MESH,
            )
            copy.start()
            self.copies[slot] = copy

    def final(self):
        total = self.chunk(self.me)
        for _, hops, base in self.ways:
            slot = base + hops - 1
            self.copies[slot].wait_recv()
            total = total + self.landed(slot)[...].astype(F32)
        return total

    def drain(self):
        for copy in self.copies.values():
            copy.wait_send()


class DirectSum:
    def __init__(self, size, me, peer, chunk, sent, landed, send_sem, recv_sem):
        self.size, self.me, self.peer, self.chunk = size, me, peer, chunk
        self.sent, self.landed = sent, landed
        self.send_sem, self.recv_sem = send_sem, recv_sem
        self.copies = []

    def stage(self, step):
        for d in range(1, self.size):
            to = lax.rem(self.me + d, self.size)
            self.sent(d - 1)[...] = self.chunk(to).astype(self.sent(d - 1).dtype)
            copy = pltpu.make_async_remote_copy(
                src_ref=self.sent(d - 1),
                dst_ref=self.landed(d - 1),
                send_sem=self.send_sem(d - 1),
                recv_sem=self.recv_sem(d - 1),
                device_id=self.peer(d),
                device_id_type=MESH,
            )
            copy.start()
            self.copies.append(copy)

    def final(self):
        total = self.chunk(self.me)
        for d, copy in enumerate(self.copies):
            copy.wait_recv()
            total = total + self.landed(d)[...].astype(F32)
        return total

    def drain(self):
        for copy in self.copies:
            copy.wait_send()


def kernel(
    q_hbm,
    g_hbm,
    x_hbm,
    k_hbm,
    v_hbm,
    act_hbm,
    w_hbm,
    len_ref,
    ada_ref,
    own_ref,
    down_ref,
    up_ref,
    qv,
    gv,
    xv,
    kv,
    bias,
    dq,
    wall,
    wz,
    act_v,
    act_cols,
    rank_cols,
    slots,
    pick_y,
    pick_x,
    meta_s,
    meta_r,
    zs,
    zr,
    eb,
    fys,
    fyr,
    fxs,
    fxr,
    sxs,
    sxr,
    sys_,
    syr,
    ty,
    tx,
    load_sem,
    kv_sem,
    wy_sem,
    wx_sem,
    wc_sem,
    wz_sem,
    z_sem,
    e_sem,
    f_sem,
    s_sem,
    m_sem,
):
    s = lax.axis_index("seq")
    z = lax.axis_index("head")
    core = lax.rem(s, 2)
    y = lax.rem(s // 2, NY)
    x = s // (2 * NY)

    def at_z(d):
        return (s, lax.rem(z + d + NZ, NZ))

    def at_y(d):
        return (x * (2 * NY) + lax.rem(y + d + NY, NY) * 2 + core, z)

    def at_x(d):
        return (lax.rem(x + d + NX, NX) * (2 * NY) + y * 2 + core, z)

    partner = (s + 1 - 2 * core, z)

    barrier = pltpu.get_barrier_semaphore()
    others = (
        [at_z(d) for d in (1, -1, 2, -2)]
        + [partner]
        + [at_y(d) for d in range(1, NY)]
        + [at_x(d) for d in range(1, NX)]
    )
    for other in others:
        pl.semaphore_signal(barrier, inc=1, device_id=other, device_id_type=MESH)

    places = (core * (NX * NY) + x * NY + y, core * (NX * NY) + y * NX + x)
    load_count = [0]

    def load(src, dst):
        copy = pltpu.make_async_copy(src, dst, load_sem.at[load_count[0]])
        load_count[0] += 1
        copy.start()
        return copy

    own_kv = []
    for g in range(KV_HEADS):
        lanes = pl.ds(g * HEAD_SIZE, HEAD_SIZE)
        own_kv.append([load(src.at[:, lanes], kv.at[HALO, g, i]) for i, src in enumerate((k_hbm, v_hbm))])
    w_load = [load(w_hbm.at[0, :, pl.ds(h * PIECE, PIECE)], wall.at[h, places[h]]) for h in range(2)]
    act_load = load(act_hbm, act_v)
    qg_load = []
    for g in range(KV_HEADS):
        lanes = pl.ds(g * GROUP * HEAD_SIZE, GROUP * HEAD_SIZE)
        qg_load.append([load(src.at[:, lanes], dst.at[:, lanes]) for src, dst in ((q_hbm, qv), (g_hbm, gv))])

    sends = []

    def remote(src, dst, sem, at, to):
        copy = pltpu.make_async_remote_copy(
            src_ref=src,
            dst_ref=dst,
            send_sem=sem.at[0, at],
            recv_sem=sem.at[1, at],
            device_id=to,
            device_id_type=MESH,
        )
        copy.start()
        sends.append(copy)
        return copy

    kv_copies = {}

    def send_kv(g, d):
        if d == 0:
            for copy in own_kv[g]:
                copy.wait()
        else:
            kv_copies[g, d].wait_recv()
        if d < HALO:
            kv_copies[g, d + 1] = remote(
                kv.at[HALO - d, g], kv.at[HALO - d - 1, g], kv_sem, g * HALO + d, at_z(1)
            )

    for copy in w_load:
        copy.wait()
    pl.semaphore_wait(barrier, len(others))

    def pass_w(h, rows, sem, at, to):
        return remote(wall.at[h, rows], wall.at[h, rows], sem, at, to)

    w_one = [
        [pass_w(0, places[0], wy_sem, d, at_y(d)) for d in range(1, NY)],
        [pass_w(1, places[1], wx_sem, d, at_x(d)) for d in range(1, NX)],
    ]
    send_kv(0, 0)
    send_kv(1, 0)

    ends, total = [], 0
    for i in range(SEGMENTS):
        total = total + len_ref[0, i]
        ends.append(total)
    starts = [0] + ends[:-1]
    lane = lax.broadcasted_iota(I32, (8, COLS), 1)
    slot = lax.rem(lane, RANK)
    for i in range(SEGMENTS):
        owner = own_ref[ada_ref[0, i]]
        slot = slot + jnp.where(lane // RANK == i, owner * RANK, 0)
    meta_s[...] = slot
    slots[:, 0:COLS] = slot
    meta = remote(meta_s, meta_r, m_sem, 0, partner)

    first = z * TOKENS
    row_pos = first + lax.broadcasted_iota(I32, (TOKENS, 1), 0)
    row_start = jnp.zeros((TOKENS, 1), I32)
    for i in range(1, SEGMENTS):
        row_start = jnp.where(row_pos >= starts[i], starts[i], row_start)
    key_pos = first - HALO * TOKENS + lax.broadcasted_iota(I32, (TOKENS, KEYS), 1)
    allowed = (key_pos >= row_start) & (key_pos <= row_pos)
    bias[...] = jnp.where(allowed, 0.0, -1e30).astype(F32)

    col = lax.broadcasted_iota(I32, (COLS, 1), 0)
    col_start = jnp.zeros((COLS, 1), I32)
    col_end = jnp.zeros((COLS, 1), I32)
    col_rows = [lax.rem(col, RANK)] * 2
    for i in range(SEGMENTS):
        here = col // RANK == i
        col_start = jnp.where(here, starts[i], col_start)
        col_end = jnp.where(here, ends[i], col_end)
        adapter = ada_ref[0, i]
        chip = adapter // 2
        for h, at in enumerate((chip, lax.rem(chip, NY) * NX + chip // NY)):
            adapter_row = (lax.rem(adapter, 2) * (NX * NY) + at) * RANK
            col_rows[h] = col_rows[h] + jnp.where(here, adapter_row, 0)
    token = first + lax.broadcasted_iota(I32, (COLS, TOKENS), 1)
    mask = (token >= col_start) & (token < col_end)
    spread = lax.rem(lax.broadcasted_iota(I32, (COLS, RANK), 0), RANK) == lax.broadcasted_iota(
        I32, (COLS, RANK), 1
    )
    spread = jnp.where(spread, 1.0, 0.0).astype(BF16)
    act_load.wait()
    act_cols[...] = jnp.where(mask, nn(spread, act_v[...]), 0.0).astype(BF16)

    def attend(g):
        for copy in qg_load[g]:
            copy.wait()
        kv_copies[g, HALO].wait_recv()

        def heads(i, carry):
            at = [
                pl.ds(pl.multiple_of((g * GROUP + PAIR * i + j) * HEAD_SIZE, HEAD_SIZE), HEAD_SIZE)
                for j in range(PAIR)
            ]
            keys = kv[:, g, 0].reshape(KEYS, HEAD_SIZE)
            values = kv[:, g, 1].reshape(KEYS, HEAD_SIZE)
            q_rows = jnp.concatenate([qv[:, lanes] for lanes in at], axis=0)
            g_rows = jnp.concatenate([gv[:, lanes] for lanes in at], axis=0)
            hidden = jnp.concatenate([bias[...]] * PAIR, axis=0)
            scores = nt(q_rows, keys) * SCORE_SCALE + hidden
            weights = jnp.exp(scores - jnp.max(scores, axis=1, keepdims=True))
            scale = 1.0 / jnp.sum(weights, axis=1, keepdims=True)
            d_prob = nt(g_rows, values)
            delta = jnp.sum(weights * d_prob, axis=1, keepdims=True) * scale
            dscore = (weights * (d_prob - delta) * (scale * SCORE_SCALE)).astype(BF16)
            grads = nn(dscore, keys).astype(BF16)
            for j in range(PAIR):
                dq[:, at[j]] = grads[j * TOKENS : (j + 1) * TOKENS]
            return carry

        lax.fori_loop(0, GROUP // PAIR, heads, 0)

    mine = core * (NX * NY)
    for copy in w_one[1]:
        copy.wait_recv()
    row = pl.ds(mine + y * NX, NX)
    w_two = [None, [pass_w(1, row, wy_sem, NY + d, at_y(d)) for d in range(1, NY)]]
    send_kv(0, 1)
    send_kv(2, 0)
    for copy in w_one[0]:
        copy.wait_recv()
    row = pl.ds(mine + x * NY, NY)
    w_two[0] = [pass_w(0, row, wx_sem, NX + d, at_x(d)) for d in range(1, NX)]
    for g, d in ((1, 1), (3, 0), (0, 2), (2, 1), (1, 2)):
        send_kv(g, d)
    meta.wait_recv()
    slots[:, COLS : 2 * COLS] = meta_r[...]
    w_core = []
    for h in range(2):
        for copy in w_two[h]:
            copy.wait_recv()
        w_core.append(pass_w(h, pl.ds(mine, NX * NY), wc_sem, h, partner))
    send_kv(3, 1)
    send_kv(2, 2)

    wz_copies = {}

    def pass_wz(h, at, origin, to):
        rows = lax.rem(z + origin + NZ, NZ)
        wz_copies[h, at] = remote(wz.at[rows, h], wz.at[rows, h], wz_sem, h * (NZ - 1) + at, at_z(to))

    def spread_near(h):
        for at, to in enumerate((2, -2, 1, -1)):
            pass_wz(h, at, 0, to)

    def spread_far(h):
        for at in range(2):
            wz_copies[h, at].wait_recv()
        pass_wz(h, 4, -2, 1)
        pass_wz(h, 5, 2, -1)
        pass_wz(h, 6, 4 * h - 2, 2 - 4 * h)

    attend(0)
    send_kv(3, 2)
    every = lax.broadcasted_iota(I32, (COLS, 2 * NX * NY * RANK), 1)
    for h in range(2):
        w_core[h].wait_recv()
        pick = jnp.where(every == col_rows[h], 1.0, 0.0).astype(BF16)
        wz[z, h] = nn(pick, wall[h].reshape(2 * NX * NY * RANK, PIECE)).astype(BF16)
        spread_near(h)
    x_load = load(x_hbm, xv)

    def fill(i, carry):
        row = i * (NX * RANK) + lax.broadcasted_iota(I32, (NX * RANK, 2 * COLS), 0)
        low = core * RANK + lax.rem(row, RANK)
        chip = row // RANK
        rows = pl.ds(pl.multiple_of(i * (NX * RANK), NX * RANK), NX * RANK)
        key = (lax.rem(chip, NX) * NY + chip // NX) * (2 * RANK) + low
        pick_y[rows, :] = jnp.where(key == slots[0:1, :], 1.0, 0.0).astype(BF16)
        pick_x[rows, :] = jnp.where(chip * (2 * RANK) + low == slots[0:1, :], 1.0, 0.0).astype(BF16)
        return carry

    lax.fori_loop(0, NY, fill, 0)
    for g in range(1, KV_HEADS):
        attend(g)
        if g == FAR:
            for h in range(2):
                spread_far(h)

    def zcols(ref, c, i, width):
        return ref[:, pl.ds(pl.multiple_of(c * width + i * PIECE, PIECE), PIECE)]

    def z_chunk(p, c):
        if p < 2:
            return nn(act_cols[...], zcols(dq, c, p, WIDTH))
        return nn(rank_cols[...], zcols(xv, c, p - 2, 2 * WIDTH))

    def y_chunk(p, c):
        rows = pl.ds(pl.multiple_of(c * (NX * RANK), NX * RANK), NX * RANK)
        return nn(pick_y[rows, :], eb[p])

    def x_chunk(p, c):
        rows = pl.ds(pl.multiple_of(c * (NY * RANK), NY * RANK), NY * RANK)
        return nn(pick_x[rows, :], eb[p])

    def rows_of(buf, c):
        return buf[pl.ds(pl.multiple_of(c * RANK, RANK), RANK), :]

    def refs(p, at, sent, landed, sem):
        return (
            lambda i: sent.at[at, i],
            lambda i: landed.at[at, i],
            lambda i: sem.at[0, p, i],
            lambda i: sem.at[1, p, i],
        )

    z_sums, f_sums, s_sums, held, e_copies = [], [], [], [], {}
    for p in range(PIECES):
        z_sums.append(
            RingSum(NZ, z, at_z, functools.partial(z_chunk, p), *refs(p, p, zs, zr, z_sem), 4 - p % 2)
        )
        at = sum((i in Y_FIRST) == (p in Y_FIRST) for i in range(p))
        if p in Y_FIRST:
            held.append(ty.at[at])
            f_sums.append(
                DirectSum(NY, y, at_y, functools.partial(y_chunk, p), *refs(p, at, fys, fyr, f_sem))
            )
            s_sums.append(
                DirectSum(NX, x, at_x, functools.partial(rows_of, ty.at[at]), *refs(p, at, sxs, sxr, s_sem))
            )
        else:
            held.append(tx.at[at])
            f_sums.append(
                DirectSum(NX, x, at_x, functools.partial(x_chunk, p), *refs(p, at, fxs, fxr, f_sem))
            )
            s_sums.append(
                DirectSum(NY, y, at_y, functools.partial(rows_of, tx.at[at]), *refs(p, at, sys_, syr, s_sem))
            )

    def to_partner(p):
        eb[p, 0:COLS] = z_sums[p].final().astype(BF16)
        e_copies[p] = remote(eb.at[p, pl.ds(0, COLS)], eb.at[p, pl.ds(COLS, COLS)], e_sem, p, partner)

    def first_hop(p):
        e_copies[p].wait_recv()
        f_sums[p].stage(0)

    def turn(p):
        held[p][...] = f_sums[p].final()
        s_sums[p].stage(0)

    def write(p):
        ref, at = (up_ref, p) if p < 2 else (down_ref, p - 2)
        ref[:, at * PIECE : (at + 1) * PIECE] = s_sums[p].final() * ADAPTER_SCALE

    def rank_all():
        rank = jnp.zeros((COLS, TOKENS), F32)
        for d, at in ((0, None), (-2, None), (2, None), (-1, 2), (1, 3), (-3, 4), (3, 5), (4, 6)):
            c = lax.rem(z + d + NZ, NZ)
            for h in range(2):
                if at is not None:
                    wz_copies[h, at].wait_recv()
                rank = rank + nt(wz[c, h], zcols(dq, c, h, WIDTH))
        rank_cols[...] = jnp.where(mask, rank, 0.0).astype(BF16)
        x_load.wait()

    plan = []
    for p, begin in enumerate(BEGIN):
        steps = [functools.partial(z_sums[p].stage, i) for i in range(4)]
        steps += [functools.partial(to_partner, p), functools.partial(first_hop, p)]
        steps += [functools.partial(turn, p), functools.partial(write, p)]
        late = (1, 2, 2) if begin == 0 else (1, 1, 1)
        when = [(begin + i, (0.5 if begin < 0 else 0, 0 if begin >= 0 else 0.5, 0 if begin >= 0 else 0.5, 0 if begin >= 0 else 0.5, 2, *late)[i]) for i in range(8)]
        if begin < 0:
            when[6:] = [(6, 3), (8, 0)]
        plan += [(*at, p, step) for at, step in zip(when, steps)]
    plan.append((0, -1, 0, rank_all))
    for _, _, _, step in sorted(plan, key=lambda entry: entry[:3]):
        step()

    for copy in sends:
        copy.wait_send()
    for sums in z_sums + f_sums + s_sums:
        sums.drain()


def on_device(q, k, v, g, x, act, w, length, adapter, owner):
    vmem = pl.BlockSpec(memory_space=pltpu.VMEM)
    smem = pl.BlockSpec(memory_space=pltpu.SMEM)
    hbm = pl.BlockSpec(memory_space=pl.ANY)
    dma = pltpu.SemaphoreType.DMA
    ring = NZ - 1
    by_y = len(Y_FIRST)
    by_x = PIECES - by_y
    features = KV_HEADS * GROUP * HEAD_SIZE
    scratch = [
        pltpu.VMEM((TOKENS, features), BF16),
        pltpu.VMEM((TOKENS, features), BF16),
        pltpu.VMEM((TOKENS, x.shape[1]), BF16),
        pltpu.VMEM((HALO + 1, KV_HEADS, 2, TOKENS, HEAD_SIZE), BF16),
        pltpu.VMEM((TOKENS, KEYS), F32),
        pltpu.VMEM((TOKENS, features), BF16),
        pltpu.VMEM((2, 2 * NX * NY, RANK, PIECE), BF16),
        pltpu.VMEM((NZ, 2, COLS, PIECE), BF16),
        pltpu.VMEM((RANK, TOKENS), BF16),
        pltpu.VMEM((COLS, TOKENS), BF16),
        pltpu.VMEM((COLS, TOKENS), BF16),
        pltpu.VMEM((8, 2 * COLS), I32),
        pltpu.VMEM((NX * NY * RANK, 2 * COLS), BF16),
        pltpu.VMEM((NX * NY * RANK, 2 * COLS), BF16),
        pltpu.VMEM((8, COLS), I32),
        pltpu.VMEM((8, COLS), I32),
        pltpu.VMEM((PIECES, ring, COLS, PIECE), BF16),
        pltpu.VMEM((PIECES, ring, COLS, PIECE), BF16),
        pltpu.VMEM((PIECES, 2 * COLS, PIECE), BF16),
        pltpu.VMEM((by_y, NY - 1, NX * RANK, PIECE), BF16),
        pltpu.VMEM((by_y, NY - 1, NX * RANK, PIECE), BF16),
        pltpu.VMEM((by_x, NX - 1, NY * RANK, PIECE), BF16),
        pltpu.VMEM((by_x, NX - 1, NY * RANK, PIECE), BF16),
        pltpu.VMEM((by_y, NX - 1, RANK, PIECE), BF16),
        pltpu.VMEM((by_y, NX - 1, RANK, PIECE), BF16),
        pltpu.VMEM((by_x, NY - 1, RANK, PIECE), BF16),
        pltpu.VMEM((by_x, NY - 1, RANK, PIECE), BF16),
        pltpu.VMEM((by_y, NX * RANK, PIECE), F32),
        pltpu.VMEM((by_x, NY * RANK, PIECE), F32),
        dma((4 * KV_HEADS + 4,)),
        dma((2, KV_HEADS * HALO)),
        dma((2, 2 * NY)),
        dma((2, 2 * NX)),
        dma((2, 2)),
        dma((2, 2 * ring)),
        dma((2, PIECES, ring)),
        dma((2, PIECES)),
        dma((2, PIECES, ring)),
        dma((2, PIECES, ring)),
        dma((2, 1)),
    ]
    down, up = pl.pallas_call(
        kernel,
        out_shape=(
            jax.ShapeDtypeStruct((RANK, 2 * WIDTH), F32),
            jax.ShapeDtypeStruct((RANK, WIDTH), F32),
        ),
        in_specs=[hbm] * 7 + [smem] * 3,
        out_specs=(vmem, vmem),
        scratch_shapes=scratch,
        compiler_params=pltpu.CompilerParams(
            collective_id=0, has_side_effects=True, vmem_limit_bytes=60 * 1024 * 1024
        ),
    )(q, g, x, k, v, act.T, w, length, adapter, owner)
    return down.T[None], up[None]


def solution(mesh):
    return jax.shard_map(
        on_device,
        mesh=mesh,
        in_specs=(
            P(("seq", "head"), None),
            P(("seq", "head"), None),
            P(("seq", "head"), None),
            P(("seq", "head"), None),
            P(("seq", "head"), None),
            P(("seq", "head"), None),
            P("seq", None, "head"),
            P("seq", None),
            P("seq", None),
            P(),
        ),
        out_specs=(P("seq", "head", None), P("seq", None, "head")),
        check_vma=False,
    )
```
